512 devices in a mesh: src: 32 (over x, z), tgt: 16 (over y, core).
Axes of the slice: x: 4, y: 8, z: 8, core: 2. Of those that a mesh axis runs over, the one named last changes fastest.
Arguments:
- source_points: bfloat16 [16, 65536], P(None, 'src'), may hold values from -8 to 8
- target_points: bfloat16 [16, 32768], P(None, 'tgt'), may hold values from -8 to 8
- source_logw: float32 [65536], P('src'), may hold values from -1 to 1
- target_logw: float32 [32768], P('tgt'), may hold values from -1 to 1
Outputs:
- pot_src: float32 [65536], P('src')
- pot_tgt: float32 [32768], P('tgt')
- row_ratio: float32 [65536], P('src')
- projected: float32 [16, 65536], P(None, 'src')
- pulled: float32 [16, 32768], P(None, 'tgt')
The draws below stay inside these ranges and needn't reach their ends.
All inputs are finite; a program needn't handle non-finite values.
Results may differ from the reference program's by a relative error of at most 0.00089.
Values sent between devices are 32-bit elements; how exact they have to be, the bound alone decides.
No kernel may reach another device: no remote copies, remote signals or barrier semaphores. Data moves between devices by JAX's collectives and lax.ppermute only.
A program may use at most 64 MiB of HBM per device.

```python
import math
import jax
import jax.numpy as jnp
from jax import lax

DIMS = 16
ITERS = 2
NS = 65536
NT = 32768


def draw_cloud(key, count):
    key_base = jax.random.fold_in(key, 0)
    values = jnp.clip(jax.random.normal(key_base, (DIMS, count), jnp.float32), -4.0, 4.0)
    return values.astype(jnp.bfloat16)


def draw_source_points(key, part):
    key = jax.random.fold_in(key, 11)
    return draw_cloud(key, NS)


def draw_target_points(key, part):
    key = jax.random.fold_in(key, 12)
    return draw_cloud(key, NT)


def level_of(own_key, shape, shards, smallest, high):
    def one(axis_at, parts):
        heights = jax.random.uniform(jax.random.fold_in(jax.random.fold_in(own_key, 6), axis_at), (parts,), jnp.float32, smallest / len(shards), high / len(shards))
        return jnp.repeat(jnp.exp(heights), shape[axis_at] // parts).reshape((-1,) + (1,) * (len(shape) - axis_at - 1))

    factor_of = one(*shards[0])
    for cut in shards[1:]:
        factor_of = factor_of * one(*cut)
    return factor_of


def setup_inputs(seed: int = 0) -> dict:
    splits = jax.random.split(jax.random.key(seed), 5)
    source_points = draw_source_points(jax.random.fold_in(splits[4], 71), 0)
    target_points = draw_target_points(jax.random.fold_in(splits[4], 71), 0)
    source_logw = jnp.clip(jax.random.uniform(splits[2], (NS,), jnp.float32, -1.0, 1.0) * level_of(splits[2], (NS,), ((0, 32),), -0.4, 0.0), -1.0, 1.0)
    target_logw = jnp.clip(jax.random.uniform(splits[3], (NT,), jnp.float32, -1.0, 1.0) * level_of(splits[3], (NT,), ((0, 16),), -0.4, 0.0), -1.0, 1.0)
    return dict(source_points=source_points, target_points=target_points, source_logw=source_logw, target_logw=target_logw)


epsilon = 0.1
far_below = -1e30


def reference(source_points, target_points, source_logw, target_logw):
    row_block = min(2048, NS)
    block_count = NS // row_block
    src_parts = source_points.reshape(DIMS, block_count, row_block).transpose(1, 0, 2)
    src_norms = jnp.sum(jnp.square(source_points.astype(jnp.float32)), axis=0).reshape(block_count, row_block)
    tgt_norms = jnp.sum(jnp.square(target_points.astype(jnp.float32)), axis=0)
    log_a = source_logw - math.log(NS)
    log_b = target_logw - math.log(NT)

    def cost_block(src_part, src_norm):
        inner_prod = lax.dot_general(src_part, target_points, (((0,), (0,)), ((), ())), preferred_element_type=jnp.float32)
        return (src_norm[:, None] + tgt_norms[None, :] - 2.0 * inner_prod) / DIMS

    def row_update(pot_tgt):
        def advance(running, inputs):
            scores = (pot_tgt[None, :] - cost_block(inputs[0], inputs[1])) / epsilon
            peaks = jnp.max(scores, axis=1)
            totals = jnp.sum(jnp.exp(scores - peaks[:, None]), axis=1)
            return running, (peaks, totals)

        _, (peaks, totals) = lax.scan(advance, jnp.zeros((), jnp.float32), (src_parts, src_norms))
        peaks = peaks.reshape(NS)
        totals = totals.reshape(NS)
        return epsilon * log_a - epsilon * (peaks + jnp.log(totals))

    def col_update(pot_src):
        pot_blocks = pot_src.reshape(block_count, row_block)

        def advance(running, inputs):
            scores = (inputs[2][:, None] - cost_block(inputs[0], inputs[1])) / epsilon
            peaks = jnp.maximum(running[0], jnp.max(scores, axis=0))
            totals = running[1] * jnp.exp(running[0] - peaks) + jnp.sum(jnp.exp(scores - peaks[None, :]), axis=0)
            return (peaks, totals), None

        start = (jnp.full((NT,), far_below, jnp.float32), jnp.zeros((NT,), jnp.float32))
        (peaks, totals), _ = lax.scan(advance, start, (src_parts, src_norms, pot_blocks))
        return epsilon * log_b - epsilon * (peaks + jnp.log(totals))

    pot_tgt = jnp.zeros((NT,), jnp.float32)
    pot_src = jnp.zeros((NS,), jnp.float32)
    for sweep in range(ITERS):
        pot_src = row_update(pot_tgt)
        pot_tgt = col_update(pot_src)

    pot_blocks = pot_src.reshape(block_count, row_block)

    def collect(running, inputs):
        coupling = jnp.exp((inputs[2][:, None] + pot_tgt[None, :] - cost_block(inputs[0], inputs[1])) / epsilon)
        row_mass = jnp.sum(coupling, axis=1)
        rounded = coupling.astype(jnp.bfloat16)
        row_sums = lax.dot_general(target_points, rounded, (((1,), (1,)), ((), ())), preferred_element_type=jnp.float32)
        col_sums = running[0] + lax.dot_general(inputs[0], rounded, (((1,), (0,)), ((), ())), preferred_element_type=jnp.float32)
        col_mass = running[1] + jnp.sum(coupling, axis=0)
        return (col_sums, col_mass), (row_sums, row_mass)

    start = (jnp.zeros((DIMS, NT), jnp.float32), jnp.zeros((NT,), jnp.float32))
    (col_sums, col_mass), (row_sums, row_mass) = lax.scan(collect, start, (src_parts, src_norms, pot_blocks))
    row_sums = row_sums.transpose(1, 0, 2).reshape(DIMS, NS)
    row_mass = row_mass.reshape(NS)
    projected = row_sums / row_mass[None, :]
    row_ratio = row_mass * jnp.exp(-log_a) - 1.0
    pulled = col_sums / col_mass[None, :]
    return (pot_src, pot_tgt, row_ratio, projected, pulled)
```

```python
import math

import jax
import jax.numpy as jnp
from jax import lax
from jax.experimental import pallas as pl
from jax.experimental.pallas import tpu as pltpu
from jax.sharding import PartitionSpec as P

EPSILON = 0.1
LOG2E = math.log2(math.e)
KAPPA = LOG2E / EPSILON
LANES = 128
GROUP = 256
CHUNK = 256
DEPTH = 64
HALF = 8


def pieces(value):
    high = value.astype(jnp.bfloat16).astype(jnp.float32)
    rest = value - high
    mid = rest.astype(jnp.bfloat16).astype(jnp.float32)
    low = (rest - mid).astype(jnp.bfloat16).astype(jnp.float32)
    return high, mid, low


def tail_rows(count, dual, dual_first):
    row = lax.broadcasted_iota(jnp.int32, (16, count), 0)
    high, mid, low = pieces(dual)
    at = 0 if dual_first else 3
    ones_at = 3 - at
    out = jnp.where((row >= ones_at) & (row < ones_at + 3), 1.0, 0.0)
    out = jnp.where(row == at, high, out)
    out = jnp.where(row == at + 1, mid, out)
    return jnp.where(row == at + 2, low, out)


def fill_operands(a_points, a_dual, b_points, b_dual, a_ref, b_ref):
    features = a_points.shape[0]
    a = a_points.astype(jnp.float32)
    cross = 2.0 * KAPPA / features
    rows = jnp.concatenate([a, a, a, tail_rows(a.shape[1], a_dual, False)], axis=0)
    a_ref[...] = rows.T.astype(jnp.bfloat16)
    high, mid, low = pieces(b_points.astype(jnp.float32) * cross)
    b_ref[...] = jnp.concatenate(
        [high, mid, low, tail_rows(high.shape[1], b_dual, True)], axis=0
    ).astype(jnp.bfloat16)


def score_chunk(a_ref, b_ref, at, group):
    return jnp.dot(
        a_ref[at : at + CHUNK, :], b_ref[:, group], preferred_element_type=jnp.float32
    )


def lse_groups(a_ref, b_ref, out_ref):
    def one(n, carry):
        group = pl.ds(pl.multiple_of(n * GROUP, GROUP), GROUP)
        peak = None
        for at in range(0, a_ref.shape[0], CHUNK):
            scores = score_chunk(a_ref, b_ref, at, group).reshape(CHUNK // 8, 8, GROUP)
            here = jnp.max(scores, axis=0)
            if peak is None:
                peak = here
                total = jnp.sum(jnp.exp2(scores - peak[None]), axis=0)
            else:
                risen = jnp.maximum(peak, here)
                total = total * jnp.exp2(peak - risen) + jnp.sum(
                    jnp.exp2(scores - risen[None]), axis=0
                )
                peak = risen
        top = jnp.max(peak, axis=0, keepdims=True)
        total = jnp.sum(total * jnp.exp2(peak - top), axis=0, keepdims=True)
        lse = top + jnp.log(total) * LOG2E
        for d in range(out_ref.shape[0]):
            out_ref[d, :, group] = lse
        return carry

    lax.fori_loop(0, b_ref.shape[1] // GROUP, one, 0)


def sum_groups(a_ref, b_ref, out_ref):
    def one(n, carry):
        group = pl.ds(pl.multiple_of(n * GROUP, GROUP), GROUP)
        total = jnp.zeros((8, GROUP), jnp.float32)
        for at in range(0, a_ref.shape[0], CHUNK):
            scores = score_chunk(a_ref, b_ref, at, group).reshape(CHUNK // 8, 8, GROUP)
            total = total + jnp.sum(jnp.exp2(scores), axis=0)
        total = jnp.sum(total, axis=0, keepdims=True)
        for d in range(out_ref.shape[0]):
            out_ref[d, :, group] = total
        return carry

    lax.fori_loop(0, b_ref.shape[1] // GROUP, one, 0)


def weighted_groups(a_ref, b_ref, points_ref, out_ref, split, exact):
    features = points_ref.shape[0]
    share = features // split

    def one(n, carry):
        group = pl.ds(pl.multiple_of(n * GROUP, GROUP), GROUP)
        total = jnp.zeros((8, GROUP), jnp.float32)
        moved = jnp.zeros((features, GROUP), jnp.float32)
        for at in range(0, a_ref.shape[0], CHUNK):
            weight = jnp.exp2(score_chunk(a_ref, b_ref, at, group))
            total = total + jnp.sum(weight.reshape(CHUNK // 8, 8, GROUP), axis=0)
            points = points_ref[:, at : at + CHUNK]
            rounded = weight.astype(jnp.bfloat16)
            moved = moved + jnp.dot(points, rounded, preferred_element_type=jnp.float32)
            if exact:
                rest = (weight - rounded.astype(jnp.float32)).astype(jnp.bfloat16)
                moved = moved + jnp.dot(points, rest, preferred_element_type=jnp.float32)
        total = jnp.sum(total, axis=0, keepdims=True)
        for part in range(GROUP // LANES):
            lanes = slice(part * LANES, (part + 1) * LANES)
            for h in range(split):
                d = (n * (GROUP // LANES) + part) * split + h
                out_ref[d, :, 0:LANES] = total[:, lanes]
                for k in range(share):
                    out_ref[d, :, (k + 1) * LANES : (k + 2) * LANES] = moved[
                        h * share + k : h * share + k + 1, lanes
                    ]
        return carry

    lax.fori_loop(0, b_ref.shape[1] // GROUP, one, 0)


def norm_of(points_ref):
    points = points_ref[...].astype(jnp.float32)
    return jnp.sum(points * points, axis=0, keepdims=True)


def joined_lse(got_ref):
    parts = [got_ref[d] for d in range(got_ref.shape[0])]
    top = parts[0]
    for part in parts[1:]:
        top = jnp.maximum(top, part)
    total = jnp.exp2(parts[0] - top)
    for part in parts[1:]:
        total = total + jnp.exp2(part - top)
    return top + jnp.log(total) * LOG2E


def joined_sum(got_ref):
    total = got_ref[0]
    for d in range(1, got_ref.shape[0]):
        total = total + got_ref[d]
    return total


def log2_weight(logw_ref, whole):
    return (logw_ref[...] - math.log(whole)) * LOG2E


def first_rows(x_ref, t_ref, out_ref, a_ref, b_ref):
    beta = norm_of(t_ref) * (-KAPPA / t_ref.shape[0])
    zero = jnp.zeros((1, x_ref.shape[1]), jnp.float32)
    fill_operands(t_ref[...], beta, x_ref[...], zero, a_ref, b_ref)
    lse_groups(a_ref, b_ref, out_ref)


def first_cols(whole, x_ref, t_ref, logw_ref, got_ref, alpha_ref, out_ref, a_ref, b_ref):
    alpha = log2_weight(logw_ref, whole) - joined_lse(got_ref)
    alpha_ref[...] = alpha
    zero = jnp.zeros((1, t_ref.shape[1]), jnp.float32)
    fill_operands(x_ref[...], alpha, t_ref[...], zero, a_ref, b_ref)
    lse_groups(a_ref, b_ref, out_ref)


def second_rows(
    whole_s, whole_t, x_ref, t_ref, slogw_ref, tlogw_ref, alpha_ref, got_ref, beta_ref, out_ref, a_ref, b_ref
):
    beta = log2_weight(tlogw_ref, whole_t) - joined_lse(got_ref)
    beta_ref[...] = beta
    over = alpha_ref[...] - log2_weight(slogw_ref, whole_s)
    fill_operands(t_ref[...], beta, x_ref[...], over, a_ref, b_ref)
    sum_groups(a_ref, b_ref, out_ref)


def second_cols(
    whole_t, x_ref, t_ref, tlogw_ref, alpha_ref, beta_ref, got_ref, alpha2_ref, out_ref, a_ref, b_ref
):
    alpha = alpha_ref[...] - jnp.log(joined_sum(got_ref)) * LOG2E
    alpha2_ref[...] = alpha
    over = beta_ref[...] - log2_weight(tlogw_ref, whole_t)
    fill_operands(x_ref[...], alpha, t_ref[...], over, a_ref, b_ref)
    weighted_groups(a_ref, b_ref, x_ref, out_ref, x_ref.shape[0] // HALF, True)


def share_means(got_ref, out_ref):
    total = joined_sum(got_ref)
    mass = total[:, :LANES]
    for d in range(out_ref.shape[0]):
        out_ref[d, :, 0:LANES] = mass
    for at in range(LANES, total.shape[1], LANES):
        mean = total[:, at : at + LANES] / mass
        for d in range(out_ref.shape[0]):
            out_ref[d, :, at : at + LANES] = mean


def unpack_means(got_ref, means_ref, split):
    features = means_ref.shape[0]
    share = features // split
    masses = []
    for d in range(got_ref.shape[0]):
        q, h = divmod(d, split)
        if h == 0:
            masses.append(got_ref[d, :, 0:LANES])
        for k in range(share):
            means_ref[h * share + k : h * share + k + 1, q * LANES : (q + 1) * LANES] = got_ref[
                d, :, (k + 1) * LANES : (k + 2) * LANES
            ]
    return jnp.concatenate(masses, axis=1)


def last_rows(
    x_ref, t_ref, alpha_ref, beta_ref, got_ref, pulled_ref, pot_tgt_ref, out_ref, a_ref, b_ref
):
    mass = unpack_means(got_ref, pulled_ref, x_ref.shape[0] // HALF)
    beta = beta_ref[...] - jnp.log(mass) * LOG2E
    pot_tgt_ref[...] = beta * (1.0 / KAPPA) + norm_of(t_ref) * (1.0 / t_ref.shape[0])
    fill_operands(t_ref[...], beta, x_ref[...], alpha_ref[...], a_ref, b_ref)
    weighted_groups(a_ref, b_ref, t_ref, out_ref, 1, False)


def finish_rows(whole, x_ref, logw_ref, alpha_ref, got_ref, projected_ref, ratio_ref, pot_src_ref):
    mass = unpack_means(got_ref, projected_ref, 1)
    ratio_ref[...] = mass * jnp.exp(math.log(whole) - logw_ref[...]) - 1.0
    pot_src_ref[...] = alpha_ref[...] * (1.0 / KAPPA) + norm_of(x_ref) * (1.0 / x_ref.shape[0])


def call(body, outs, *args, operands=None):
    scratch = []
    if operands is not None:
        scratch = [
            pltpu.VMEM((operands[0], DEPTH), jnp.bfloat16),
            pltpu.VMEM((DEPTH, operands[1]), jnp.bfloat16),
        ]
    return pl.pallas_call(
        body,
        out_shape=[jax.ShapeDtypeStruct(shape, jnp.float32) for shape in outs],
        scratch_shapes=scratch,
        compiler_params=pltpu.CompilerParams(vmem_limit_bytes=32 * 1024 * 1024),
    )(*args)


def spread(parts, axis):
    return lax.all_to_all(parts, axis, 0, 0, tiled=True)


def per_device(x, t, source_logw, target_logw):
    features, rows = x.shape
    cols = t.shape[1]
    n_src, n_tgt = lax.axis_size("src"), lax.axis_size("tgt")
    whole_s, whole_t = rows * n_src, cols * n_tgt
    slogw = source_logw.reshape(1, rows)
    tlogw = target_logw.reshape(1, cols)
    split = features // HALF
    assert n_src * LANES == cols * split and n_tgt * LANES == rows
    col_row = (n_src, 1, (HALF + 1) * LANES)
    row_row = (n_tgt, 1, (features + 1) * LANES)
    by_row, by_col = (cols, rows), (rows, cols)

    (lse,) = call(first_rows, [(n_tgt, 1, rows)], x, t, operands=by_row)
    got = spread(lse, "tgt")

    def body(*refs):
        first_cols(whole_s, *refs)

    alpha, lse = call(body, [(1, rows), (n_src, 1, cols)], x, t, slogw, got, operands=by_col)
    got = spread(lse, "src")

    def body(*refs):
        second_rows(whole_s, whole_t, *refs)

    beta, mass = call(
        body, [(1, cols), (n_tgt, 1, rows)], x, t, slogw, tlogw, alpha, got, operands=by_row
    )
    got = spread(mass, "tgt")

    def body(*refs):
        second_cols(whole_t, *refs)

    alpha, sums = call(
        body, [(1, rows), col_row], x, t, tlogw, alpha, beta, got, operands=by_col
    )
    got = spread(sums, "src")
    (means,) = call(share_means, [col_row], got)
    got = spread(means, "src")
    pulled, pot_tgt, sums = call(
        last_rows, [(features, cols), (1, cols), row_row], x, t, alpha, beta, got, operands=by_row
    )
    got = spread(sums, "tgt")
    (means,) = call(share_means, [row_row], got)
    got = spread(means, "tgt")

    def body(*refs):
        finish_rows(whole_s, *refs)

    projected, ratio, pot_src = call(
        body, [(features, rows), (1, rows), (1, rows)], x, slogw, alpha, got
    )
    return (pot_src.reshape(rows), pot_tgt.reshape(cols), ratio.reshape(rows), projected, pulled)


def solution(mesh):
    in_specs = (P(None, "src"), P(None, "tgt"), P("src"), P("tgt"))
    out_specs = (P("src"), P("tgt"), P("src"), P(None, "src"), P(None, "tgt"))
    return jax.shard_map(
        per_device, mesh=mesh, in_specs=in_specs, out_specs=out_specs, check_vma=False
    )
```

```python
import math

import jax
import jax.numpy as jnp
from jax import lax
from jax.experimental import pallas as pl
from jax.experimental.pallas import tpu as pltpu
from jax.sharding import PartitionSpec as P

EPSILON = 0.1
LOG2E = math.log2(math.e)
KAPPA = LOG2E / EPSILON
LANES = 128
CHUNK = 256
LSE_CHUNK = 64
DEPTH = 64
HALF = 8


def pieces(value):
    high = value.astype(jnp.bfloat16).astype(jnp.float32)
    rest = value - high
    mid = rest.astype(jnp.bfloat16).astype(jnp.float32)
    low = (rest - mid).astype(jnp.bfloat16).astype(jnp.float32)
    return high, mid, low


def tail_rows(count, dual, dual_first):
    row = lax.broadcasted_iota(jnp.int32, (16, count), 0)
    high, mid, low = pieces(dual)
    at = 0 if dual_first else 3
    ones_at = 3 - at
    out = jnp.where((row >= ones_at) & (row < ones_at + 3), 1.0, 0.0)
    out = jnp.where(row == at, high, out)
    out = jnp.where(row == at + 1, mid, out)
    return jnp.where(row == at + 2, low, out)


def fill_operands(a_points, a_dual, b_points, b_dual, a_ref, b_ref):
    features = a_points.shape[0]
    a = a_points.astype(jnp.float32)
    cross = 2.0 * KAPPA / features
    rows = jnp.concatenate([a, a, a, tail_rows(a.shape[1], a_dual, False)], axis=0)
    a_ref[...] = rows.T.astype(jnp.bfloat16)
    high, mid, low = pieces(b_points.astype(jnp.float32) * cross)
    b_ref[...] = jnp.concatenate(
        [high, mid, low, tail_rows(high.shape[1], b_dual, True)], axis=0
    ).astype(jnp.bfloat16)


def score_chunk(a_ref, b_ref, at, count):
    return jnp.dot(a_ref[at : at + count, :], b_ref[...], preferred_element_type=jnp.float32)


def by_sublane(array):
    return array.reshape(array.shape[0] // 8, 8, array.shape[1])


def lse_columns(a_ref, b_ref, out_ref):
    peak = None
    for at in range(0, a_ref.shape[0], LSE_CHUNK):
        scores = by_sublane(score_chunk(a_ref, b_ref, at, LSE_CHUNK))
        here = jnp.max(scores, axis=0)
        if peak is None:
            peak = here
            total = jnp.sum(jnp.exp2(scores - peak[None]), axis=0)
        else:
            risen = jnp.maximum(peak, here)
            total = total * jnp.exp2(peak - risen) + jnp.sum(
                jnp.exp2(scores - risen[None]), axis=0
            )
            peak = risen
    top = jnp.max(peak, axis=0, keepdims=True)
    total = jnp.sum(total * jnp.exp2(peak - top), axis=0, keepdims=True)
    lse = top + jnp.log(total) * LOG2E
    for d in range(out_ref.shape[0]):
        out_ref[d] = lse


def sum_columns(a_ref, b_ref, out_ref):
    total = jnp.zeros((8, b_ref.shape[1]), jnp.float32)
    for at in range(0, a_ref.shape[0], CHUNK):
        total = total + jnp.sum(by_sublane(jnp.exp2(score_chunk(a_ref, b_ref, at, CHUNK))), axis=0)
    total = jnp.sum(total, axis=0, keepdims=True)
    for d in range(out_ref.shape[0]):
        out_ref[d] = total


def weighted_columns(a_ref, b_ref, points_ref, out_ref, split, exact):
    features = points_ref.shape[0]
    share = features // split
    cols = b_ref.shape[1]
    total = jnp.zeros((8, cols), jnp.float32)
    moved = jnp.zeros((features, cols), jnp.float32)
    for at in range(0, a_ref.shape[0], CHUNK):
        weight = jnp.exp2(score_chunk(a_ref, b_ref, at, CHUNK))
        total = total + jnp.sum(by_sublane(weight), axis=0)
        points = points_ref[:, at : at + CHUNK]
        rounded = weight.astype(jnp.bfloat16)
        moved = moved + jnp.dot(points, rounded, preferred_element_type=jnp.float32)
        if exact:
            rest = (weight - rounded.astype(jnp.float32)).astype(jnp.bfloat16)
            moved = moved + jnp.dot(points, rest, preferred_element_type=jnp.float32)
    total = jnp.sum(total, axis=0, keepdims=True)
    for q in range(cols // LANES):
        lanes = slice(q * LANES, (q + 1) * LANES)
        for h in range(split):
            d = q * split + h
            out_ref[d, :, 0:LANES] = total[:, lanes]
            for k in range(share):
                out_ref[d, :, (k + 1) * LANES : (k + 2) * LANES] = moved[
                    h * share + k : h * share + k + 1, lanes
                ]


def norm_of(points_ref):
    points = points_ref[...].astype(jnp.float32)
    return jnp.sum(points * points, axis=0, keepdims=True)


def joined_lse(got_ref):
    parts = [got_ref[d] for d in range(got_ref.shape[0])]
    top = parts[0]
    for part in parts[1:]:
        top = jnp.maximum(top, part)
    total = jnp.exp2(parts[0] - top)
    for part in parts[1:]:
        total = total + jnp.exp2(part - top)
    return top + jnp.log(total) * LOG2E


def joined_sum(got_ref):
    total = got_ref[0]
    for d in range(1, got_ref.shape[0]):
        total = total + got_ref[d]
    return total


def log2_weight(logw_ref, whole):
    return (logw_ref[...] - math.log(whole)) * LOG2E


def first_rows(x_ref, t_ref, out_ref, a_ref, b_ref):
    beta = norm_of(t_ref) * (-KAPPA / t_ref.shape[0])
    zero = jnp.zeros((1, x_ref.shape[1]), jnp.float32)
    fill_operands(t_ref[...], beta, x_ref[...], zero, a_ref, b_ref)
    lse_columns(a_ref, b_ref, out_ref)


def first_cols(whole, x_ref, t_ref, logw_ref, got_ref, alpha_ref, out_ref, a_ref, b_ref):
    alpha = log2_weight(logw_ref, whole) - joined_lse(got_ref)
    alpha_ref[...] = alpha
    zero = jnp.zeros((1, t_ref.shape[1]), jnp.float32)
    fill_operands(x_ref[...], alpha, t_ref[...], zero, a_ref, b_ref)
    lse_columns(a_ref, b_ref, out_ref)


def second_rows(
    whole_s, whole_t, x_ref, t_ref, slogw_ref, tlogw_ref, alpha_ref, got_ref, beta_ref, out_ref, a_ref, b_ref
):
    beta = log2_weight(tlogw_ref, whole_t) - joined_lse(got_ref)
    beta_ref[...] = beta
    over = alpha_ref[...] - log2_weight(slogw_ref, whole_s)
    fill_operands(t_ref[...], beta, x_ref[...], over, a_ref, b_ref)
    sum_columns(a_ref, b_ref, out_ref)


def second_cols(
    whole_t, x_ref, t_ref, tlogw_ref, alpha_ref, beta_ref, got_ref, alpha2_ref, out_ref, a_ref, b_ref
):
    alpha = alpha_ref[...] - jnp.log(joined_sum(got_ref)) * LOG2E
    alpha2_ref[...] = alpha
    over = beta_ref[...] - log2_weight(tlogw_ref, whole_t)
    fill_operands(x_ref[...], alpha, t_ref[...], over, a_ref, b_ref)
    weighted_columns(a_ref, b_ref, x_ref, out_ref, x_ref.shape[0] // HALF, True)


def share_means(got_ref, out_ref):
    total = joined_sum(got_ref)
    mass = total[:, :LANES]
    for d in range(out_ref.shape[0]):
        out_ref[d, :, 0:LANES] = mass
    for at in range(LANES, total.shape[1], LANES):
        mean = total[:, at : at + LANES] / mass
        for d in range(out_ref.shape[0]):
            out_ref[d, :, at : at + LANES] = mean


def unpack_means(got_ref, means_ref, split):
    features = means_ref.shape[0]
    share = features // split
    masses = []
    for d in range(got_ref.shape[0]):
        q, h = divmod(d, split)
        if h == 0:
            masses.append(got_ref[d, :, 0:LANES])
        for k in range(share):
            means_ref[h * share + k : h * share + k + 1, q * LANES : (q + 1) * LANES] = got_ref[
                d, :, (k + 1) * LANES : (k + 2) * LANES
            ]
    return jnp.concatenate(masses, axis=1)


def last_rows(
    x_ref, t_ref, alpha_ref, beta_ref, got_ref, pulled_ref, pot_tgt_ref, out_ref, a_ref, b_ref
):
    mass = unpack_means(got_ref, pulled_ref, x_ref.shape[0] // HALF)
    beta = beta_ref[...] - jnp.log(mass) * LOG2E
    pot_tgt_ref[...] = beta * (1.0 / KAPPA) + norm_of(t_ref) * (1.0 / t_ref.shape[0])
    fill_operands(t_ref[...], beta, x_ref[...], alpha_ref[...], a_ref, b_ref)
    weighted_columns(a_ref, b_ref, t_ref, out_ref, 1, False)


def finish_rows(whole, x_ref, logw_ref, alpha_ref, got_ref, projected_ref, ratio_ref, pot_src_ref):
    mass = unpack_means(got_ref, projected_ref, 1)
    ratio_ref[...] = mass * jnp.exp(math.log(whole) - logw_ref[...]) - 1.0
    pot_src_ref[...] = alpha_ref[...] * (1.0 / KAPPA) + norm_of(x_ref) * (1.0 / x_ref.shape[0])


def call(body, outs, *args, operands=None):
    scratch = []
    if operands is not None:
        scratch = [
            pltpu.VMEM((operands[0], DEPTH), jnp.bfloat16),
            pltpu.VMEM((DEPTH, operands[1]), jnp.bfloat16),
        ]
    return pl.pallas_call(
        body,
        out_shape=[jax.ShapeDtypeStruct(shape, jnp.float32) for shape in outs],
        scratch_shapes=scratch,
        compiler_params=pltpu.CompilerParams(vmem_limit_bytes=48 * 1024 * 1024),
    )(*args)


def spread(parts, axis):
    return lax.all_to_all(parts, axis, 0, 0, tiled=True)


def per_device(x, t, source_logw, target_logw):
    features, rows = x.shape
    cols = t.shape[1]
    n_src, n_tgt = lax.axis_size("src"), lax.axis_size("tgt")
    whole_s, whole_t = rows * n_src, cols * n_tgt
    slogw = source_logw.reshape(1, rows)
    tlogw = target_logw.reshape(1, cols)
    split = features // HALF
    assert n_src * LANES == cols * split and n_tgt * LANES == rows
    col_row = (n_src, 1, (HALF + 1) * LANES)
    row_row = (n_tgt, 1, (features + 1) * LANES)
    by_row, by_col = (cols, rows), (rows, cols)

    (lse,) = call(first_rows, [(n_tgt, 1, rows)], x, t, operands=by_row)
    got = spread(lse, "tgt")

    def body(*refs):
        first_cols(whole_s, *refs)

    alpha, lse = call(body, [(1, rows), (n_src, 1, cols)], x, t, slogw, got, operands=by_col)
    got = spread(lse, "src")

    def body(*refs):
        second_rows(whole_s, whole_t, *refs)

    beta, mass = call(
        body, [(1, cols), (n_tgt, 1, rows)], x, t, slogw, tlogw, alpha, got, operands=by_row
    )
    got = spread(mass, "tgt")

    def body(*refs):
        second_cols(whole_t, *refs)

    alpha, sums = call(
        body, [(1, rows), col_row], x, t, tlogw, alpha, beta, got, operands=by_col
    )
    got = spread(sums, "src")
    (means,) = call(share_means, [col_row], got)
    got = spread(means, "src")
    pulled, pot_tgt, sums = call(
        last_rows, [(features, cols), (1, cols), row_row], x, t, alpha, beta, got, operands=by_row
    )
    got = spread(sums, "tgt")
    (means,) = call(share_means, [row_row], got)
    got = spread(means, "tgt")

    def body(*refs):
        finish_rows(whole_s, *refs)

    projected, ratio, pot_src = call(
        body, [(features, rows), (1, rows), (1, rows)], x, slogw, alpha, got
    )
    return (pot_src.reshape(rows), pot_tgt.reshape(cols), ratio.reshape(rows), projected, pulled)


def solution(mesh):
    in_specs = (P(None, "src"), P(None, "tgt"), P("src"), P("tgt"))
    out_specs = (P("src"), P("tgt"), P("src"), P(None, "src"), P(None, "tgt"))
    return jax.shard_map(
        per_device, mesh=mesh, in_specs=in_specs, out_specs=out_specs, check_vma=False
    )
```

```python
import math

import jax
import jax.numpy as jnp
from jax import lax
from jax.experimental import pallas as pl
from jax.experimental.pallas import tpu as pltpu
from jax.sharding import PartitionSpec as P

EPSILON = 0.1
LOG2E = math.log2(math.e)
KAPPA = LOG2E / EPSILON
LANES = 128
CHUNK = 256
LSE_CHUNK = 64
DEPTH = 64
HALF = 8
INNER = 8
SAFE = 2.0**-80


def pieces(value):
    high = value.astype(jnp.bfloat16).astype(jnp.float32)
    rest = value - high
    mid = rest.astype(jnp.bfloat16).astype(jnp.float32)
    low = (rest - mid).astype(jnp.bfloat16).astype(jnp.float32)
    return high, mid, low


def tail_rows(count, dual, dual_first):
    row = lax.broadcasted_iota(jnp.int32, (16, count), 0)
    high, mid, low = pieces(dual)
    at = 0 if dual_first else 3
    ones_at = 3 - at
    out = jnp.where((row >= ones_at) & (row < ones_at + 3), 1.0, 0.0)
    out = jnp.where(row == at, high, out)
    out = jnp.where(row == at + 1, mid, out)
    return jnp.where(row == at + 2, low, out)


def fill_operands(a_points, a_dual, b_points, b_dual, a_ref, b_ref):
    features = a_points.shape[0]
    a = a_points.astype(jnp.float32)
    cross = 2.0 * KAPPA / features
    rows = jnp.concatenate([a, a, a, tail_rows(a.shape[1], a_dual, False)], axis=0)
    a_ref[...] = rows.T.astype(jnp.bfloat16)
    high, mid, low = pieces(b_points.astype(jnp.float32) * cross)
    b_ref[...] = jnp.concatenate(
        [high, mid, low, tail_rows(high.shape[1], b_dual, True)], axis=0
    ).astype(jnp.bfloat16)


def score_chunk(a_ref, b_ref, at, count):
    return jnp.dot(a_ref[at : at + count, :], b_ref[...], preferred_element_type=jnp.float32)


def by_sublane(array):
    return array.reshape(array.shape[0] // 8, 8, array.shape[1])


def lse_columns(a_ref, b_ref, b_dual, out_ref):
    def store(lse):
        for d in range(out_ref.shape[0]):
            out_ref[d] = lse - b_dual

    total = total_of(a_ref, b_ref)
    store(jnp.log(total) * LOG2E)

    @pl.when(jnp.min(total) < SAFE)
    def with_peaks():
        store(lse_of(a_ref, b_ref))


def lse_of(a_ref, b_ref):
    peak = None
    for at in range(0, a_ref.shape[0], LSE_CHUNK):
        scores = by_sublane(score_chunk(a_ref, b_ref, at, LSE_CHUNK))
        here = jnp.max(scores, axis=0)
        if peak is None:
            peak = here
            total = jnp.sum(jnp.exp2(scores - peak[None]), axis=0)
        else:
            risen = jnp.maximum(peak, here)
            total = total * jnp.exp2(peak - risen) + jnp.sum(
                jnp.exp2(scores - risen[None]), axis=0
            )
            peak = risen
    top = jnp.max(peak, axis=0, keepdims=True)
    total = jnp.sum(total * jnp.exp2(peak - top), axis=0, keepdims=True)
    return top + jnp.log(total) * LOG2E


def total_of(a_ref, b_ref):
    total = jnp.zeros((8, b_ref.shape[1]), jnp.float32)
    for at in range(0, a_ref.shape[0], CHUNK):
        total = total + jnp.sum(by_sublane(jnp.exp2(score_chunk(a_ref, b_ref, at, CHUNK))), axis=0)
    return jnp.sum(total, axis=0, keepdims=True)


def sum_columns(a_ref, b_ref, out_ref):
    total = total_of(a_ref, b_ref)
    for d in range(out_ref.shape[0]):
        out_ref[d] = total


def weighted_columns(a_ref, b_ref, points_ref, out_ref, split, exact):
    features = points_ref.shape[0]
    share = features // split
    cols = b_ref.shape[1]
    total = jnp.zeros((8, cols), jnp.float32)
    moved = jnp.zeros((features, cols), jnp.float32)
    for at in range(0, a_ref.shape[0], CHUNK):
        weight = jnp.exp2(score_chunk(a_ref, b_ref, at, CHUNK))
        total = total + jnp.sum(by_sublane(weight), axis=0)
        points = points_ref[:, at : at + CHUNK]
        rounded = weight.astype(jnp.bfloat16)
        moved = moved + jnp.dot(points, rounded, preferred_element_type=jnp.float32)
        if exact:
            rest = (weight - rounded.astype(jnp.float32)).astype(jnp.bfloat16)
            moved = moved + jnp.dot(points, rest, preferred_element_type=jnp.float32)
    total = jnp.sum(total, axis=0, keepdims=True)
    for q in range(cols // LANES):
        lanes = slice(q * LANES, (q + 1) * LANES)
        for h in range(split):
            d = q * split + h
            out_ref[d, :, 0:LANES] = total[:, lanes]
            for k in range(share):
                out_ref[d, :, (k + 1) * LANES : (k + 2) * LANES] = moved[
                    h * share + k : h * share + k + 1, lanes
                ]


def norm_of(points_ref):
    points = points_ref[...].astype(jnp.float32)
    return jnp.sum(points * points, axis=0, keepdims=True)


def joined_lse(got_ref):
    parts = [got_ref[d] for d in range(got_ref.shape[0])]
    top = parts[0]
    for part in parts[1:]:
        top = jnp.maximum(top, part)
    total = jnp.exp2(parts[0] - top)
    for part in parts[1:]:
        total = total + jnp.exp2(part - top)
    return top + jnp.log(total) * LOG2E


def joined_sum(got_ref):
    total = got_ref[0]
    for d in range(1, got_ref.shape[0]):
        total = total + got_ref[d]
    return total


def log2_weight(logw_ref, whole):
    return (logw_ref[...] - math.log(whole)) * LOG2E


def norm_dual(points_ref):
    return norm_of(points_ref) * (-KAPPA / points_ref.shape[0])


def first_rows(x_ref, t_ref, out_ref, a_ref, b_ref):
    over = norm_dual(x_ref)
    fill_operands(t_ref[...], norm_dual(t_ref), x_ref[...], over, a_ref, b_ref)
    lse_columns(a_ref, b_ref, over, out_ref)


def first_cols(whole, x_ref, t_ref, logw_ref, got_ref, alpha_ref, out_ref, a_ref, b_ref):
    alpha = log2_weight(logw_ref, whole) - joined_lse(got_ref)
    alpha_ref[...] = alpha
    over = norm_dual(t_ref)
    fill_operands(x_ref[...], alpha, t_ref[...], over, a_ref, b_ref)
    lse_columns(a_ref, b_ref, over, out_ref)


def second_rows(
    whole_s, whole_t, x_ref, t_ref, slogw_ref, tlogw_ref, alpha_ref, got_ref, beta_ref, out_ref, a_ref, b_ref
):
    beta = log2_weight(tlogw_ref, whole_t) - joined_lse(got_ref)
    beta_ref[...] = beta
    over = alpha_ref[...] - log2_weight(slogw_ref, whole_s)
    fill_operands(t_ref[...], beta, x_ref[...], over, a_ref, b_ref)
    sum_columns(a_ref, b_ref, out_ref)


def second_cols(
    whole_t, x_ref, t_ref, tlogw_ref, alpha_ref, beta_ref, got_ref, alpha2_ref, out_ref, a_ref, b_ref
):
    alpha = alpha_ref[...] - jnp.log(joined_sum(got_ref)) * LOG2E
    alpha2_ref[...] = alpha
    over = beta_ref[...] - log2_weight(tlogw_ref, whole_t)
    fill_operands(x_ref[...], alpha, t_ref[...], over, a_ref, b_ref)
    weighted_columns(a_ref, b_ref, x_ref, out_ref, x_ref.shape[0] // HALF, True)


def share_means(got_ref, out_ref):
    total = joined_sum(got_ref)
    mass = total[:, :LANES]
    for d in range(out_ref.shape[0]):
        out_ref[d, :, 0:LANES] = mass
    for at in range(LANES, total.shape[1], LANES):
        mean = total[:, at : at + LANES] / mass
        for d in range(out_ref.shape[0]):
            out_ref[d, :, at : at + LANES] = mean


def unpack_means(got_ref, means_ref, split):
    features = means_ref.shape[0]
    share = features // split
    masses = []
    for d in range(got_ref.shape[0]):
        q, h = divmod(d, split)
        if h == 0:
            masses.append(got_ref[d, :, 0:LANES])
        for k in range(share):
            means_ref[h * share + k : h * share + k + 1, q * LANES : (q + 1) * LANES] = got_ref[
                d, :, (k + 1) * LANES : (k + 2) * LANES
            ]
    return jnp.concatenate(masses, axis=1)


def last_rows(
    x_ref, t_ref, alpha_ref, beta_ref, got_ref, pulled_ref, pot_tgt_ref, out_ref, a_ref, b_ref
):
    mass = unpack_means(got_ref, pulled_ref, x_ref.shape[0] // HALF)
    beta = beta_ref[...] - jnp.log(mass) * LOG2E
    pot_tgt_ref[...] = beta * (1.0 / KAPPA) + norm_of(t_ref) * (1.0 / t_ref.shape[0])
    fill_operands(t_ref[...], beta, x_ref[...], alpha_ref[...], a_ref, b_ref)
    weighted_columns(a_ref, b_ref, t_ref, out_ref, 1, False)


def finish_rows(whole, x_ref, logw_ref, alpha_ref, got_ref, projected_ref, ratio_ref, pot_src_ref):
    mass = unpack_means(got_ref, projected_ref, 1)
    ratio_ref[...] = mass * jnp.exp(math.log(whole) - logw_ref[...]) - 1.0
    pot_src_ref[...] = alpha_ref[...] * (1.0 / KAPPA) + norm_of(x_ref) * (1.0 / x_ref.shape[0])


def call(body, outs, *args, operands=None):
    scratch = []
    if operands is not None:
        scratch = [
            pltpu.VMEM((operands[0], DEPTH), jnp.bfloat16),
            pltpu.VMEM((DEPTH, operands[1]), jnp.bfloat16),
        ]
    return pl.pallas_call(
        body,
        out_shape=[jax.ShapeDtypeStruct(shape, jnp.float32) for shape in outs],
        scratch_shapes=scratch,
        compiler_params=pltpu.CompilerParams(vmem_limit_bytes=48 * 1024 * 1024),
    )(*args)


def spread(parts, axis, order=None):
    groups = None if order is None else [order]
    return lax.all_to_all(parts, axis, 0, 0, axis_index_groups=groups, tiled=True)


def per_device(x, t, source_logw, target_logw):
    features, rows = x.shape
    cols = t.shape[1]
    n_src, n_tgt = lax.axis_size("src"), lax.axis_size("tgt")
    whole_s, whole_t = rows * n_src, cols * n_tgt
    slogw = source_logw.reshape(1, rows)
    tlogw = target_logw.reshape(1, cols)
    split = features // HALF
    order = [(r % (n_src // INNER)) * INNER + r // (n_src // INNER) for r in range(n_src)]
    assert n_src * LANES == cols * split and n_tgt * LANES == rows
    col_row = (n_src, 1, (HALF + 1) * LANES)
    row_row = (n_tgt, 1, (features + 1) * LANES)
    by_row, by_col = (cols, rows), (rows, cols)

    (lse,) = call(first_rows, [(n_tgt, 1, rows)], x, t, operands=by_row)
    got = spread(lse, "tgt")

    def body(*refs):
        first_cols(whole_s, *refs)

    alpha, lse = call(body, [(1, rows), (n_src, 1, cols)], x, t, slogw, got, operands=by_col)
    got = spread(lse, "src", order)

    def body(*refs):
        second_rows(whole_s, whole_t, *refs)

    beta, mass = call(
        body, [(1, cols), (n_tgt, 1, rows)], x, t, slogw, tlogw, alpha, got, operands=by_row
    )
    got = spread(mass, "tgt")

    def body(*refs):
        second_cols(whole_t, *refs)

    alpha, sums = call(
        body, [(1, rows), col_row], x, t, tlogw, alpha, beta, got, operands=by_col
    )
    got = spread(sums, "src", order)
    (means,) = call(share_means, [col_row], got)
    got = spread(means, "src", order)
    pulled, pot_tgt, sums = call(
        last_rows, [(features, cols), (1, cols), row_row], x, t, alpha, beta, got, operands=by_row
    )
    got = spread(sums, "tgt")
    (means,) = call(share_means, [row_row], got)
    got = spread(means, "tgt")

    def body(*refs):
        finish_rows(whole_s, *refs)

    projected, ratio, pot_src = call(
        body, [(features, rows), (1, rows), (1, rows)], x, slogw, alpha, got
    )
    return (pot_src.reshape(rows), pot_tgt.reshape(cols), ratio.reshape(rows), projected, pulled)


def solution(mesh):
    in_specs = (P(None, "src"), P(None, "tgt"), P("src"), P("tgt"))
    out_specs = (P("src"), P("tgt"), P("src"), P(None, "src"), P(None, "tgt"))
    return jax.shard_map(
        per_device, mesh=mesh, in_specs=in_specs, out_specs=out_specs, check_vma=False
    )
```

```python
import math

import jax
import jax.numpy as jnp
from jax import lax
from jax.experimental import pallas as pl
from jax.experimental.pallas import tpu as pltpu
from jax.sharding import PartitionSpec as P

EPSILON = 0.1
LOG2E = math.log2(math.e)
KAPPA = LOG2E / EPSILON
LANES = 128
CHUNK = 256
LSE_CHUNK = 64
DEPTH = 64
HALF = 8
INNER = 8
FIRST = 5
SAFE = 2.0**-80


def pieces(value):
    high = value.astype(jnp.bfloat16).astype(jnp.float32)
    rest = value - high
    mid = rest.astype(jnp.bfloat16).astype(jnp.float32)
    low = (rest - mid).astype(jnp.bfloat16).astype(jnp.float32)
    return high, mid, low


def tail_rows(count, dual, dual_first):
    row = lax.broadcasted_iota(jnp.int32, (16, count), 0)
    high, mid, low = pieces(dual)
    at = 0 if dual_first else 3
    ones_at = 3 - at
    out = jnp.where((row >= ones_at) & (row < ones_at + 3), 1.0, 0.0)
    out = jnp.where(row == at, high, out)
    out = jnp.where(row == at + 1, mid, out)
    return jnp.where(row == at + 2, low, out)


def fill_operands(a_points, a_dual, b_points, b_dual, a_ref, b_ref):
    features = a_points.shape[0]
    a = a_points.astype(jnp.float32)
    cross = 2.0 * KAPPA / features
    rows = jnp.concatenate([a, a, a, tail_rows(a.shape[1], a_dual, False)], axis=0)
    a_ref[...] = rows.T.astype(jnp.bfloat16)
    high, mid, low = pieces(b_points.astype(jnp.float32) * cross)
    b_ref[...] = jnp.concatenate(
        [high, mid, low, tail_rows(high.shape[1], b_dual, True)], axis=0
    ).astype(jnp.bfloat16)


def score_chunk(a_ref, b_ref, at, count):
    return jnp.dot(a_ref[at : at + count, :], b_ref[...], preferred_element_type=jnp.float32)


def by_sublane(array):
    return array.reshape(array.shape[0] // 8, 8, array.shape[1])


def lse_columns(a_ref, b_ref, b_dual, out_ref):
    def store(lse):
        for d in range(out_ref.shape[0]):
            out_ref[d] = lse - b_dual

    total = total_of(a_ref, b_ref)
    store(jnp.log(total) * LOG2E)

    @pl.when(jnp.min(total) < SAFE)
    def with_peaks():
        store(lse_of(a_ref, b_ref))


def lse_of(a_ref, b_ref):
    peak = None
    for at in range(0, a_ref.shape[0], LSE_CHUNK):
        scores = by_sublane(score_chunk(a_ref, b_ref, at, LSE_CHUNK))
        here = jnp.max(scores, axis=0)
        if peak is None:
            peak = here
            total = jnp.sum(jnp.exp2(scores - peak[None]), axis=0)
        else:
            risen = jnp.maximum(peak, here)
            total = total * jnp.exp2(peak - risen) + jnp.sum(
                jnp.exp2(scores - risen[None]), axis=0
            )
            peak = risen
    top = jnp.max(peak, axis=0, keepdims=True)
    total = jnp.sum(total * jnp.exp2(peak - top), axis=0, keepdims=True)
    return top + jnp.log(total) * LOG2E


def total_of(a_ref, b_ref):
    total = jnp.zeros((8, b_ref.shape[1]), jnp.float32)
    for at in range(0, a_ref.shape[0], CHUNK):
        total = total + jnp.sum(by_sublane(jnp.exp2(score_chunk(a_ref, b_ref, at, CHUNK))), axis=0)
    return jnp.sum(total, axis=0, keepdims=True)


def sum_columns(a_ref, b_ref, out_ref):
    total = total_of(a_ref, b_ref)
    for d in range(out_ref.shape[0]):
        out_ref[d] = total


def weighted_columns(a_ref, b_ref, points_ref, out_ref, split, exact):
    features = points_ref.shape[0]
    share = features // split
    cols = b_ref.shape[1]
    total = jnp.zeros((8, cols), jnp.float32)
    moved = jnp.zeros((features, cols), jnp.float32)
    for at in range(0, a_ref.shape[0], CHUNK):
        weight = jnp.exp2(score_chunk(a_ref, b_ref, at, CHUNK))
        total = total + jnp.sum(by_sublane(weight), axis=0)
        points = points_ref[:, at : at + CHUNK]
        rounded = weight.astype(jnp.bfloat16)
        moved = moved + jnp.dot(points, rounded, preferred_element_type=jnp.float32)
        if exact:
            rest = (weight - rounded.astype(jnp.float32)).astype(jnp.bfloat16)
            moved = moved + jnp.dot(points, rest, preferred_element_type=jnp.float32)
    total = jnp.sum(total, axis=0, keepdims=True)
    for q in range(cols // LANES):
        lanes = slice(q * LANES, (q + 1) * LANES)
        for h in range(split):
            d = q * split + h
            out_ref[d, :, 0:LANES] = total[:, lanes]
            for k in range(share):
                out_ref[d, :, (k + 1) * LANES : (k + 2) * LANES] = moved[
                    h * share + k : h * share + k + 1, lanes
                ]


def norm_of(points_ref):
    points = points_ref[...].astype(jnp.float32)
    return jnp.sum(points * points, axis=0, keepdims=True)


def joined_lse(got_ref):
    parts = [got_ref[d] for d in range(got_ref.shape[0])]
    top = parts[0]
    for part in parts[1:]:
        top = jnp.maximum(top, part)
    total = jnp.exp2(parts[0] - top)
    for part in parts[1:]:
        total = total + jnp.exp2(part - top)
    return top + jnp.log(total) * LOG2E


def joined_sum(got_ref):
    total = got_ref[0]
    for d in range(1, got_ref.shape[0]):
        total = total + got_ref[d]
    return total


def log2_weight(logw_ref, whole):
    return (logw_ref[...] - math.log(whole)) * LOG2E


def norm_dual(points_ref):
    return norm_of(points_ref) * (-KAPPA / points_ref.shape[0])


def first_rows(x_ref, t_ref, out_ref, a_ref, b_ref):
    over = norm_dual(x_ref)
    fill_operands(t_ref[...], norm_dual(t_ref), x_ref[...], over, a_ref, b_ref)
    lse_columns(a_ref, b_ref, over, out_ref)


def first_cols(whole, x_ref, t_ref, logw_ref, got_ref, alpha_ref, out_ref, a_ref, b_ref):
    alpha = log2_weight(logw_ref, whole) - joined_lse(got_ref)
    alpha_ref[...] = alpha
    over = norm_dual(t_ref)
    fill_operands(x_ref[...], alpha, t_ref[...], over, a_ref, b_ref)
    lse_columns(a_ref, b_ref, over, out_ref)


def second_rows(
    whole_s, whole_t, x_ref, t_ref, slogw_ref, tlogw_ref, alpha_ref, got_ref, beta_ref, out_ref, a_ref, b_ref
):
    beta = log2_weight(tlogw_ref, whole_t) - joined_lse(got_ref)
    beta_ref[...] = beta
    over = alpha_ref[...] - log2_weight(slogw_ref, whole_s)
    fill_operands(t_ref[...], beta, x_ref[...], over, a_ref, b_ref)
    sum_columns(a_ref, b_ref, out_ref)


def second_cols(
    whole_t, x_ref, t_ref, tlogw_ref, alpha_ref, beta_ref, got_ref, alpha2_ref, out_ref, a_ref, b_ref
):
    alpha = alpha_ref[...] - jnp.log(joined_sum(got_ref)) * LOG2E
    alpha2_ref[...] = alpha
    over = beta_ref[...] - log2_weight(tlogw_ref, whole_t)
    fill_operands(x_ref[...], alpha, t_ref[...], over, a_ref, b_ref)
    weighted_columns(a_ref, b_ref, x_ref, out_ref, x_ref.shape[0] // HALF, True)


def share_means(got_ref, out_ref):
    total = joined_sum(got_ref)
    mass = total[:, :LANES]
    for d in range(out_ref.shape[0]):
        out_ref[d, :, 0:LANES] = mass
    for at in range(LANES, total.shape[1], LANES):
        mean = total[:, at : at + LANES] / mass
        for d in range(out_ref.shape[0]):
            out_ref[d, :, at : at + LANES] = mean


def unpack_means(got_ref, means_ref, split):
    features = means_ref.shape[0]
    share = features // split
    masses = []
    for d in range(got_ref.shape[0]):
        q, h = divmod(d, split)
        if h == 0:
            masses.append(got_ref[d, :, 0:LANES])
        for k in range(share):
            means_ref[h * share + k : h * share + k + 1, q * LANES : (q + 1) * LANES] = got_ref[
                d, :, (k + 1) * LANES : (k + 2) * LANES
            ]
    return jnp.concatenate(masses, axis=1)


def last_rows(
    x_ref, t_ref, alpha_ref, beta_ref, got_ref, pulled_ref, pot_tgt_ref, out_ref, a_ref, b_ref
):
    mass = unpack_means(got_ref, pulled_ref, x_ref.shape[0] // HALF)
    beta = beta_ref[...] - jnp.log(mass) * LOG2E
    pot_tgt_ref[...] = beta * (1.0 / KAPPA) + norm_of(t_ref) * (1.0 / t_ref.shape[0])
    fill_operands(t_ref[...], beta, x_ref[...], alpha_ref[...], a_ref, b_ref)
    weighted_columns(a_ref, b_ref, t_ref, out_ref, 1, False)


def finish_rows(whole, x_ref, logw_ref, alpha_ref, got_ref, projected_ref, ratio_ref, pot_src_ref):
    mass = unpack_means(got_ref, projected_ref, 1)
    ratio_ref[...] = mass * jnp.exp(math.log(whole) - logw_ref[...]) - 1.0
    pot_src_ref[...] = alpha_ref[...] * (1.0 / KAPPA) + norm_of(x_ref) * (1.0 / x_ref.shape[0])


def call(body, outs, *args, operands=None):
    scratch = []
    if operands is not None:
        scratch = [
            pltpu.VMEM((operands[0], DEPTH), jnp.bfloat16),
            pltpu.VMEM((DEPTH, operands[1]), jnp.bfloat16),
        ]
    return pl.pallas_call(
        body,
        out_shape=[jax.ShapeDtypeStruct(shape, jnp.float32) for shape in outs],
        scratch_shapes=scratch,
        compiler_params=pltpu.CompilerParams(vmem_limit_bytes=48 * 1024 * 1024),
    )(*args)


def spread(parts, axis, order):
    return lax.all_to_all(parts, axis, 0, 0, axis_index_groups=[order], tiled=True)


def per_device(x, t, source_logw, target_logw):
    features, rows = x.shape
    cols = t.shape[1]
    n_src, n_tgt = lax.axis_size("src"), lax.axis_size("tgt")
    whole_s, whole_t = rows * n_src, cols * n_tgt
    slogw = source_logw.reshape(1, rows)
    tlogw = target_logw.reshape(1, cols)
    split = features // HALF
    outer = n_src // INNER
    by_src = [(r + outer // 2) % outer * INNER + (r // outer + FIRST) % INNER for r in range(n_src)]
    by_tgt = [(r + n_tgt // 2) % n_tgt for r in range(n_tgt)]
    assert n_src * LANES == cols * split and n_tgt * LANES == rows
    col_row = (n_src, 1, (HALF + 1) * LANES)
    row_row = (n_tgt, 1, (features + 1) * LANES)
    by_row, by_col = (cols, rows), (rows, cols)

    (lse,) = call(first_rows, [(n_tgt, 1, rows)], x, t, operands=by_row)
    got = spread(lse, "tgt", by_tgt)

    def body(*refs):
        first_cols(whole_s, *refs)

    alpha, lse = call(body, [(1, rows), (n_src, 1, cols)], x, t, slogw, got, operands=by_col)
    got = spread(lse, "src", by_src)

    def body(*refs):
        second_rows(whole_s, whole_t, *refs)

    beta, mass = call(
        body, [(1, cols), (n_tgt, 1, rows)], x, t, slogw, tlogw, alpha, got, operands=by_row
    )
    got = spread(mass, "tgt", by_tgt)

    def body(*refs):
        second_cols(whole_t, *refs)

    alpha, sums = call(
        body, [(1, rows), col_row], x, t, tlogw, alpha, beta, got, operands=by_col
    )
    got = spread(sums, "src", by_src)
    (means,) = call(share_means, [col_row], got)
    got = spread(means, "src", by_src)
    pulled, pot_tgt, sums = call(
        last_rows, [(features, cols), (1, cols), row_row], x, t, alpha, beta, got, operands=by_row
    )
    got = spread(sums, "tgt", by_tgt)
    (means,) = call(share_means, [row_row], got)
    got = spread(means, "tgt", by_tgt)

    def body(*refs):
        finish_rows(whole_s, *refs)

    projected, ratio, pot_src = call(
        body, [(features, rows), (1, rows), (1, rows)], x, slogw, alpha, got
    )
    return (pot_src.reshape(rows), pot_tgt.reshape(cols), ratio.reshape(rows), projected, pulled)


def solution(mesh):
    in_specs = (P(None, "src"), P(None, "tgt"), P("src"), P("tgt"))
    out_specs = (P("src"), P("tgt"), P("src"), P(None, "src"), P(None, "tgt"))
    return jax.shard_map(
        per_device, mesh=mesh, in_specs=in_specs, out_specs=out_specs, check_vma=False
    )
```

```python
import math

import jax
import jax.numpy as jnp
from jax import lax
from jax.experimental import pallas as pl
from jax.experimental.pallas import tpu as pltpu
from jax.sharding import PartitionSpec as P

EPSILON = 0.1
LOG2E = math.log2(math.e)
KAPPA = LOG2E / EPSILON
LANES = 128
CHUNK = 256
LSE_CHUNK = 64
DEPTH = 64
HALF = 8
INNER = 8
FIRST = 5
SAFE = 2.0**-80


def pieces(value):
    high = value.astype(jnp.bfloat16).astype(jnp.float32)
    rest = value - high
    mid = rest.astype(jnp.bfloat16).astype(jnp.float32)
    low = (rest - mid).astype(jnp.bfloat16).astype(jnp.float32)
    return high, mid, low


def tail_rows(count, dual, dual_first):
    row = lax.broadcasted_iota(jnp.int32, (16, count), 0)
    high, mid, low = pieces(dual)
    at = 0 if dual_first else 3
    ones_at = 3 - at
    out = jnp.where((row >= ones_at) & (row < ones_at + 3), 1.0, 0.0)
    out = jnp.where(row == at, high, out)
    out = jnp.where(row == at + 1, mid, out)
    return jnp.where(row == at + 2, low, out)


def fill_operands(a_points, a_dual, b_points, b_dual, a_ref, b_ref):
    features = a_points.shape[0]
    a = a_points.astype(jnp.float32)
    cross = 2.0 * KAPPA / features
    rows = jnp.concatenate([a, a, a, tail_rows(a.shape[1], a_dual, False)], axis=0)
    a_ref[...] = rows.T.astype(jnp.bfloat16)
    high, mid, low = pieces(b_points.astype(jnp.float32) * cross)
    b_ref[...] = jnp.concatenate(
        [high, mid, low, tail_rows(high.shape[1], b_dual, True)], axis=0
    ).astype(jnp.bfloat16)


def score_chunk(a_ref, b_ref, at, count):
    return jnp.dot(a_ref[at : at + count, :], b_ref[...], preferred_element_type=jnp.float32)


def by_sublane(array):
    return array.reshape(array.shape[0] // 8, 8, array.shape[1])


def lse_columns(a_ref, b_ref, b_dual, out_ref):
    def store(lse):
        for d in range(out_ref.shape[0]):
            out_ref[d] = lse - b_dual

    total = total_of(a_ref, b_ref)
    store(jnp.log(total) * LOG2E)

    @pl.when(jnp.min(total) < SAFE)
    def with_peaks():
        store(lse_of(a_ref, b_ref))


def lse_of(a_ref, b_ref):
    peak = None
    for at in range(0, a_ref.shape[0], LSE_CHUNK):
        scores = by_sublane(score_chunk(a_ref, b_ref, at, LSE_CHUNK))
        here = jnp.max(scores, axis=0)
        if peak is None:
            peak = here
            total = jnp.sum(jnp.exp2(scores - peak[None]), axis=0)
        else:
            risen = jnp.maximum(peak, here)
            total = total * jnp.exp2(peak - risen) + jnp.sum(
                jnp.exp2(scores - risen[None]), axis=0
            )
            peak = risen
    top = jnp.max(peak, axis=0, keepdims=True)
    total = jnp.sum(total * jnp.exp2(peak - top), axis=0, keepdims=True)
    return top + jnp.log(total) * LOG2E


def total_of(a_ref, b_ref):
    total = jnp.zeros((8, b_ref.shape[1]), jnp.float32)
    for at in range(0, a_ref.shape[0], CHUNK):
        total = total + jnp.sum(by_sublane(jnp.exp2(score_chunk(a_ref, b_ref, at, CHUNK))), axis=0)
    return jnp.sum(total, axis=0, keepdims=True)


def sum_columns(a_ref, b_ref, out_ref):
    total = total_of(a_ref, b_ref)
    for d in range(out_ref.shape[0]):
        out_ref[d] = total


def weighted_columns(a_ref, b_ref, points_ref, out_ref, split, exact):
    features = points_ref.shape[0]
    share = features // split
    cols = b_ref.shape[1]
    total = jnp.zeros((8, cols), jnp.float32)
    moved = jnp.zeros((features, cols), jnp.float32)
    for at in range(0, a_ref.shape[0], CHUNK):
        weight = jnp.exp2(score_chunk(a_ref, b_ref, at, CHUNK))
        total = total + jnp.sum(by_sublane(weight), axis=0)
        points = points_ref[:, at : at + CHUNK]
        rounded = weight.astype(jnp.bfloat16)
        moved = moved + jnp.dot(points, rounded, preferred_element_type=jnp.float32)
        if exact:
            rest = (weight - rounded.astype(jnp.float32)).astype(jnp.bfloat16)
            moved = moved + jnp.dot(points, rest, preferred_element_type=jnp.float32)
    total = jnp.sum(total, axis=0, keepdims=True)
    for q in range(cols // LANES):
        lanes = slice(q * LANES, (q + 1) * LANES)
        for h in range(split):
            d = q * split + h
            out_ref[d, :, 0:LANES] = total[:, lanes]
            for k in range(share):
                out_ref[d, :, (k + 1) * LANES : (k + 2) * LANES] = moved[
                    h * share + k : h * share + k + 1, lanes
                ]


def norm_of(points_ref):
    points = points_ref[...].astype(jnp.float32)
    return jnp.sum(points * points, axis=0, keepdims=True)


def joined_lse(got_ref):
    parts = [got_ref[d] for d in range(got_ref.shape[0])]
    top = parts[0]
    for part in parts[1:]:
        top = jnp.maximum(top, part)
    total = jnp.exp2(parts[0] - top)
    for part in parts[1:]:
        total = total + jnp.exp2(part - top)
    return top + jnp.log(total) * LOG2E


def joined_sum(got_ref):
    total = got_ref[0]
    for d in range(1, got_ref.shape[0]):
        total = total + got_ref[d]
    return total


def log2_weight(logw_ref, whole):
    return (logw_ref[...] - math.log(whole)) * LOG2E


def clouds(xt_ref):
    features = xt_ref.shape[0] // 2
    return xt_ref.at[:features], xt_ref.at[features:]


def norm_dual(points_ref):
    return norm_of(points_ref) * (-KAPPA / points_ref.shape[0])


def first_rows(xt_ref, out_ref, a_ref, b_ref):
    x_ref, t_ref = clouds(xt_ref)
    over = norm_dual(x_ref)
    fill_operands(t_ref[...], norm_dual(t_ref), x_ref[...], over, a_ref, b_ref)
    lse_columns(a_ref, b_ref, over, out_ref)


def first_cols(whole, xt_ref, logw_ref, got_ref, alpha_ref, out_ref, a_ref, b_ref):
    x_ref, t_ref = clouds(xt_ref)
    alpha = log2_weight(logw_ref, whole) - joined_lse(got_ref)
    alpha_ref[...] = alpha
    over = norm_dual(t_ref)
    fill_operands(x_ref[...], alpha, t_ref[...], over, a_ref, b_ref)
    lse_columns(a_ref, b_ref, over, out_ref)


def second_rows(
    whole_s, whole_t, xt_ref, slogw_ref, tlogw_ref, alpha_ref, got_ref, beta_ref, out_ref, a_ref, b_ref
):
    x_ref, t_ref = clouds(xt_ref)
    beta = log2_weight(tlogw_ref, whole_t) - joined_lse(got_ref)
    beta_ref[...] = beta
    over = alpha_ref[...] - log2_weight(slogw_ref, whole_s)
    fill_operands(t_ref[...], beta, x_ref[...], over, a_ref, b_ref)
    sum_columns(a_ref, b_ref, out_ref)


def second_cols(
    whole_t, xt_ref, tlogw_ref, alpha_ref, beta_ref, got_ref, alpha2_ref, out_ref, a_ref, b_ref
):
    x_ref, t_ref = clouds(xt_ref)
    alpha = alpha_ref[...] - jnp.log(joined_sum(got_ref)) * LOG2E
    alpha2_ref[...] = alpha
    over = beta_ref[...] - log2_weight(tlogw_ref, whole_t)
    fill_operands(x_ref[...], alpha, t_ref[...], over, a_ref, b_ref)
    weighted_columns(a_ref, b_ref, x_ref, out_ref, x_ref.shape[0] // HALF, True)


def share_means(got_ref, out_ref):
    total = joined_sum(got_ref)
    mass = total[:, :LANES]
    for d in range(out_ref.shape[0]):
        out_ref[d, :, 0:LANES] = mass
    for at in range(LANES, total.shape[1], LANES):
        mean = total[:, at : at + LANES] / mass
        for d in range(out_ref.shape[0]):
            out_ref[d, :, at : at + LANES] = mean


def unpack_means(got_ref, means_ref, split):
    features = means_ref.shape[0]
    share = features // split
    masses = []
    for d in range(got_ref.shape[0]):
        q, h = divmod(d, split)
        if h == 0:
            masses.append(got_ref[d, :, 0:LANES])
        for k in range(share):
            means_ref[h * share + k : h * share + k + 1, q * LANES : (q + 1) * LANES] = got_ref[
                d, :, (k + 1) * LANES : (k + 2) * LANES
            ]
    return jnp.concatenate(masses, axis=1)


def last_rows(
    xt_ref, alpha_ref, beta_ref, got_ref, pulled_ref, pot_tgt_ref, out_ref, a_ref, b_ref
):
    x_ref, t_ref = clouds(xt_ref)
    mass = unpack_means(got_ref, pulled_ref, x_ref.shape[0] // HALF)
    beta = beta_ref[...] - jnp.log(mass) * LOG2E
    pot_tgt_ref[...] = beta * (1.0 / KAPPA) + norm_of(t_ref) * (1.0 / t_ref.shape[0])
    fill_operands(t_ref[...], beta, x_ref[...], alpha_ref[...], a_ref, b_ref)
    weighted_columns(a_ref, b_ref, t_ref, out_ref, 1, False)


def finish_rows(whole, xt_ref, logw_ref, alpha_ref, got_ref, projected_ref, ratio_ref, pot_src_ref):
    x_ref, _ = clouds(xt_ref)
    mass = unpack_means(got_ref, projected_ref, 1)
    ratio_ref[...] = mass * jnp.exp(math.log(whole) - logw_ref[...]) - 1.0
    pot_src_ref[...] = alpha_ref[...] * (1.0 / KAPPA) + norm_of(x_ref) * (1.0 / x_ref.shape[0])


def call(body, outs, *args, operands=None):
    scratch = []
    if operands is not None:
        scratch = [
            pltpu.VMEM((operands[0], DEPTH), jnp.bfloat16),
            pltpu.VMEM((DEPTH, operands[1]), jnp.bfloat16),
        ]
    return pl.pallas_call(
        body,
        out_shape=[jax.ShapeDtypeStruct(shape, jnp.float32) for shape in outs],
        scratch_shapes=scratch,
        compiler_params=pltpu.CompilerParams(vmem_limit_bytes=48 * 1024 * 1024),
    )(*args)


def spread(parts, axis, order):
    return lax.all_to_all(parts, axis, 0, 0, axis_index_groups=[order], tiled=True)


def per_device(x, t, source_logw, target_logw):
    features, rows = x.shape
    cols = t.shape[1]
    n_src, n_tgt = lax.axis_size("src"), lax.axis_size("tgt")
    whole_s, whole_t = rows * n_src, cols * n_tgt
    slogw = source_logw.reshape(1, rows)
    tlogw = target_logw.reshape(1, cols)
    split = features // HALF
    xt = jnp.concatenate([x, t], axis=0)
    outer = n_src // INNER
    by_src = [(r + outer // 2) % outer * INNER + (r // outer + FIRST) % INNER for r in range(n_src)]
    by_tgt = [(r + n_tgt // 2) % n_tgt for r in range(n_tgt)]
    assert rows == cols and n_src * LANES == cols * split and n_tgt * LANES == rows
    col_row = (n_src, 1, (HALF + 1) * LANES)
    row_row = (n_tgt, 1, (features + 1) * LANES)
    by_row, by_col = (cols, rows), (rows, cols)

    (lse,) = call(first_rows, [(n_tgt, 1, rows)], xt, operands=by_row)
    got = spread(lse, "tgt", by_tgt)

    def body(*refs):
        first_cols(whole_s, *refs)

    alpha, lse = call(body, [(1, rows), (n_src, 1, cols)], xt, slogw, got, operands=by_col)
    got = spread(lse, "src", by_src)

    def body(*refs):
        second_rows(whole_s, whole_t, *refs)

    beta, mass = call(
        body, [(1, cols), (n_tgt, 1, rows)], xt, slogw, tlogw, alpha, got, operands=by_row
    )
    got = spread(mass, "tgt", by_tgt)

    def body(*refs):
        second_cols(whole_t, *refs)

    alpha, sums = call(
        body, [(1, rows), col_row], xt, tlogw, alpha, beta, got, operands=by_col
    )
    got = spread(sums, "src", by_src)
    (means,) = call(share_means, [col_row], got)
    got = spread(means, "src", by_src)
    pulled, pot_tgt, sums = call(
        last_rows, [(features, cols), (1, cols), row_row], xt, alpha, beta, got, operands=by_row
    )
    got = spread(sums, "tgt", by_tgt)
    (means,) = call(share_means, [row_row], got)
    got = spread(means, "tgt", by_tgt)

    def body(*refs):
        finish_rows(whole_s, *refs)

    projected, ratio, pot_src = call(
        body, [(features, rows), (1, rows), (1, rows)], xt, slogw, alpha, got
    )
    return (pot_src.reshape(rows), pot_tgt.reshape(cols), ratio.reshape(rows), projected, pulled)


def solution(mesh):
    in_specs = (P(None, "src"), P(None, "tgt"), P("src"), P("tgt"))
    out_specs = (P("src"), P("tgt"), P("src"), P(None, "src"), P(None, "tgt"))
    return jax.shard_map(
        per_device, mesh=mesh, in_specs=in_specs, out_specs=out_specs, check_vma=False
    )
```

```python
import math

import jax
import jax.numpy as jnp
from jax import lax
from jax.experimental import pallas as pl
from jax.experimental.pallas import tpu as pltpu
from jax.sharding import PartitionSpec as P

EPSILON = 0.1
LOG2E = math.log2(math.e)
KAPPA = LOG2E / EPSILON
LANES = 128
CHUNK = 256
LSE_CHUNK = 64
DEPTH = 64
HALF = 8
INNER = 8
FIRST = 5
STRIDE = 3
SAFE = 2.0**-80


def pieces(value):
    high = value.astype(jnp.bfloat16).astype(jnp.float32)
    rest = value - high
    mid = rest.astype(jnp.bfloat16).astype(jnp.float32)
    low = (rest - mid).astype(jnp.bfloat16).astype(jnp.float32)
    return high, mid, low


def tail_rows(count, dual, dual_first):
    row = lax.broadcasted_iota(jnp.int32, (16, count), 0)
    high, mid, low = pieces(dual)
    at = 0 if dual_first else 3
    ones_at = 3 - at
    out = jnp.where((row >= ones_at) & (row < ones_at + 3), 1.0, 0.0)
    out = jnp.where(row == at, high, out)
    out = jnp.where(row == at + 1, mid, out)
    return jnp.where(row == at + 2, low, out)


def fill_operands(a_points, a_dual, b_points, b_dual, a_ref, b_ref):
    features = a_points.shape[0]
    a = a_points.astype(jnp.float32)
    cross = 2.0 * KAPPA / features
    rows = jnp.concatenate([a, a, a, tail_rows(a.shape[1], a_dual, False)], axis=0)
    a_ref[...] = rows.T.astype(jnp.bfloat16)
    high, mid, low = pieces(b_points.astype(jnp.float32) * cross)
    b_ref[...] = jnp.concatenate(
        [high, mid, low, tail_rows(high.shape[1], b_dual, True)], axis=0
    ).astype(jnp.bfloat16)


def score_chunk(a_ref, b_ref, at, count):
    return jnp.dot(a_ref[at : at + count, :], b_ref[...], preferred_element_type=jnp.float32)


def by_sublane(array):
    return array.reshape(array.shape[0] // 8, 8, array.shape[1])


def lse_columns(a_ref, b_ref, b_dual, out_ref):
    def store(lse):
        for d in range(out_ref.shape[0]):
            out_ref[d] = lse - b_dual

    total = total_of(a_ref, b_ref)
    store(jnp.log(total) * LOG2E)

    @pl.when(jnp.min(total) < SAFE)
    def with_peaks():
        store(lse_of(a_ref, b_ref))


def lse_of(a_ref, b_ref):
    peak = None
    for at in range(0, a_ref.shape[0], LSE_CHUNK):
        scores = by_sublane(score_chunk(a_ref, b_ref, at, LSE_CHUNK))
        here = jnp.max(scores, axis=0)
        if peak is None:
            peak = here
            total = jnp.sum(jnp.exp2(scores - peak[None]), axis=0)
        else:
            risen = jnp.maximum(peak, here)
            total = total * jnp.exp2(peak - risen) + jnp.sum(
                jnp.exp2(scores - risen[None]), axis=0
            )
            peak = risen
    top = jnp.max(peak, axis=0, keepdims=True)
    total = jnp.sum(total * jnp.exp2(peak - top), axis=0, keepdims=True)
    return top + jnp.log(total) * LOG2E


def total_of(a_ref, b_ref):
    total = jnp.zeros((8, b_ref.shape[1]), jnp.float32)
    for at in range(0, a_ref.shape[0], CHUNK):
        total = total + jnp.sum(by_sublane(jnp.exp2(score_chunk(a_ref, b_ref, at, CHUNK))), axis=0)
    return jnp.sum(total, axis=0, keepdims=True)


def sum_columns(a_ref, b_ref, out_ref):
    total = total_of(a_ref, b_ref)
    for d in range(out_ref.shape[0]):
        out_ref[d] = total


def weighted_columns(a_ref, b_ref, points_ref, out_ref, split, exact):
    features = points_ref.shape[0]
    share = features // split
    cols = b_ref.shape[1]
    total = jnp.zeros((8, cols), jnp.float32)
    moved = jnp.zeros((features, cols), jnp.float32)
    for at in range(0, a_ref.shape[0], CHUNK):
        weight = jnp.exp2(score_chunk(a_ref, b_ref, at, CHUNK))
        total = total + jnp.sum(by_sublane(weight), axis=0)
        points = points_ref[:, at : at + CHUNK]
        rounded = weight.astype(jnp.bfloat16)
        moved = moved + jnp.dot(points, rounded, preferred_element_type=jnp.float32)
        if exact:
            rest = (weight - rounded.astype(jnp.float32)).astype(jnp.bfloat16)
            moved = moved + jnp.dot(points, rest, preferred_element_type=jnp.float32)
    total = jnp.sum(total, axis=0, keepdims=True)
    for q in range(cols // LANES):
        lanes = slice(q * LANES, (q + 1) * LANES)
        for h in range(split):
            d = q * split + h
            out_ref[d, :, 0:LANES] = total[:, lanes]
            for k in range(share):
                out_ref[d, :, (k + 1) * LANES : (k + 2) * LANES] = moved[
                    h * share + k : h * share + k + 1, lanes
                ]


def norm_of(points_ref):
    points = points_ref[...].astype(jnp.float32)
    return jnp.sum(points * points, axis=0, keepdims=True)


def joined_lse(got_ref):
    parts = [got_ref[d] for d in range(got_ref.shape[0])]
    top = parts[0]
    for part in parts[1:]:
        top = jnp.maximum(top, part)
    total = jnp.exp2(parts[0] - top)
    for part in parts[1:]:
        total = total + jnp.exp2(part - top)
    return top + jnp.log(total) * LOG2E


def joined_sum(got_ref):
    total = got_ref[0]
    for d in range(1, got_ref.shape[0]):
        total = total + got_ref[d]
    return total


def log2_weight(logw_ref, whole):
    return (logw_ref[...] - math.log(whole)) * LOG2E


def clouds(xt_ref):
    features = xt_ref.shape[0] // 2
    return xt_ref.at[:features], xt_ref.at[features:]


def norm_dual(points_ref):
    return norm_of(points_ref) * (-KAPPA / points_ref.shape[0])


def first_rows(xt_ref, out_ref, a_ref, b_ref):
    x_ref, t_ref = clouds(xt_ref)
    over = norm_dual(x_ref)
    fill_operands(t_ref[...], norm_dual(t_ref), x_ref[...], over, a_ref, b_ref)
    lse_columns(a_ref, b_ref, over, out_ref)


def first_cols(whole, xt_ref, logw_ref, got_ref, alpha_ref, out_ref, a_ref, b_ref):
    x_ref, t_ref = clouds(xt_ref)
    alpha = log2_weight(logw_ref, whole) - joined_lse(got_ref)
    alpha_ref[...] = alpha
    over = norm_dual(t_ref)
    fill_operands(x_ref[...], alpha, t_ref[...], over, a_ref, b_ref)
    lse_columns(a_ref, b_ref, over, out_ref)


def second_rows(
    whole_s, whole_t, xt_ref, slogw_ref, tlogw_ref, alpha_ref, got_ref, beta_ref, out_ref, a_ref, b_ref
):
    x_ref, t_ref = clouds(xt_ref)
    beta = log2_weight(tlogw_ref, whole_t) - joined_lse(got_ref)
    beta_ref[...] = beta
    over = alpha_ref[...] - log2_weight(slogw_ref, whole_s)
    fill_operands(t_ref[...], beta, x_ref[...], over, a_ref, b_ref)
    sum_columns(a_ref, b_ref, out_ref)


def second_cols(
    whole_t, xt_ref, tlogw_ref, alpha_ref, beta_ref, got_ref, alpha2_ref, out_ref, a_ref, b_ref
):
    x_ref, t_ref = clouds(xt_ref)
    alpha = alpha_ref[...] - jnp.log(joined_sum(got_ref)) * LOG2E
    alpha2_ref[...] = alpha
    over = beta_ref[...] - log2_weight(tlogw_ref, whole_t)
    fill_operands(x_ref[...], alpha, t_ref[...], over, a_ref, b_ref)
    weighted_columns(a_ref, b_ref, x_ref, out_ref, x_ref.shape[0] // HALF, True)


def share_means(got_ref, out_ref):
    total = joined_sum(got_ref)
    mass = total[:, :LANES]
    for d in range(out_ref.shape[0]):
        out_ref[d, :, 0:LANES] = mass
    for at in range(LANES, total.shape[1], LANES):
        mean = total[:, at : at + LANES] / mass
        for d in range(out_ref.shape[0]):
            out_ref[d, :, at : at + LANES] = mean


def unpack_means(got_ref, means_ref, split):
    features = means_ref.shape[0]
    share = features // split
    masses = []
    for d in range(got_ref.shape[0]):
        q, h = divmod(d, split)
        if h == 0:
            masses.append(got_ref[d, :, 0:LANES])
        for k in range(share):
            means_ref[h * share + k : h * share + k + 1, q * LANES : (q + 1) * LANES] = got_ref[
                d, :, (k + 1) * LANES : (k + 2) * LANES
            ]
    return jnp.concatenate(masses, axis=1)


def last_rows(
    xt_ref, alpha_ref, beta_ref, got_ref, pulled_ref, pot_tgt_ref, out_ref, a_ref, b_ref
):
    x_ref, t_ref = clouds(xt_ref)
    mass = unpack_means(got_ref, pulled_ref, x_ref.shape[0] // HALF)
    beta = beta_ref[...] - jnp.log(mass) * LOG2E
    pot_tgt_ref[...] = beta * (1.0 / KAPPA) + norm_of(t_ref) * (1.0 / t_ref.shape[0])
    fill_operands(t_ref[...], beta, x_ref[...], alpha_ref[...], a_ref, b_ref)
    weighted_columns(a_ref, b_ref, t_ref, out_ref, 1, False)


def finish_rows(whole, xt_ref, logw_ref, alpha_ref, got_ref, projected_ref, ratio_ref, pot_src_ref):
    x_ref, _ = clouds(xt_ref)
    mass = unpack_means(got_ref, projected_ref, 1)
    ratio_ref[...] = mass * jnp.exp(math.log(whole) - logw_ref[...]) - 1.0
    pot_src_ref[...] = alpha_ref[...] * (1.0 / KAPPA) + norm_of(x_ref) * (1.0 / x_ref.shape[0])


def call(body, outs, *args, operands=None):
    scratch = []
    if operands is not None:
        scratch = [
            pltpu.VMEM((operands[0], DEPTH), jnp.bfloat16),
            pltpu.VMEM((DEPTH, operands[1]), jnp.bfloat16),
        ]
    return pl.pallas_call(
        body,
        out_shape=[jax.ShapeDtypeStruct(shape, jnp.float32) for shape in outs],
        scratch_shapes=scratch,
        compiler_params=pltpu.CompilerParams(vmem_limit_bytes=48 * 1024 * 1024),
    )(*args)


def spread(parts, axis, order):
    return lax.all_to_all(parts, axis, 0, 0, axis_index_groups=[order], tiled=True)


def per_device(x, t, source_logw, target_logw):
    features, rows = x.shape
    cols = t.shape[1]
    n_src, n_tgt = lax.axis_size("src"), lax.axis_size("tgt")
    whole_s, whole_t = rows * n_src, cols * n_tgt
    slogw = source_logw.reshape(1, rows)
    tlogw = target_logw.reshape(1, cols)
    split = features // HALF
    xt = jnp.concatenate([x, t], axis=0)
    outer = n_src // INNER
    by_src = [(r + outer // 2) % outer * INNER + (r // outer + FIRST) % INNER for r in range(n_src)]
    by_tgt = [(STRIDE * r + n_tgt // 2) % n_tgt for r in range(n_tgt)]
    assert rows == cols and n_src * LANES == cols * split and n_tgt * LANES == rows
    col_row = (n_src, 1, (HALF + 1) * LANES)
    row_row = (n_tgt, 1, (features + 1) * LANES)
    by_row, by_col = (cols, rows), (rows, cols)

    (lse,) = call(first_rows, [(n_tgt, 1, rows)], xt, operands=by_row)
    got = spread(lse, "tgt", by_tgt)

    def body(*refs):
        first_cols(whole_s, *refs)

    alpha, lse = call(body, [(1, rows), (n_src, 1, cols)], xt, slogw, got, operands=by_col)
    got = spread(lse, "src", by_src)

    def body(*refs):
        second_rows(whole_s, whole_t, *refs)

    beta, mass = call(
        body, [(1, cols), (n_tgt, 1, rows)], xt, slogw, tlogw, alpha, got, operands=by_row
    )
    got = spread(mass, "tgt", by_tgt)

    def body(*refs):
        second_cols(whole_t, *refs)

    alpha, sums = call(
        body, [(1, rows), col_row], xt, tlogw, alpha, beta, got, operands=by_col
    )
    got = spread(sums, "src", by_src)
    (means,) = call(share_means, [col_row], got)
    got = spread(means, "src", by_src)
    pulled, pot_tgt, sums = call(
        last_rows, [(features, cols), (1, cols), row_row], xt, alpha, beta, got, operands=by_row
    )
    got = spread(sums, "tgt", by_tgt)
    (means,) = call(share_means, [row_row], got)
    got = spread(means, "tgt", by_tgt)

    def body(*refs):
        finish_rows(whole_s, *refs)

    projected, ratio, pot_src = call(
        body, [(features, rows), (1, rows), (1, rows)], xt, slogw, alpha, got
    )
    return (pot_src.reshape(rows), pot_tgt.reshape(cols), ratio.reshape(rows), projected, pulled)


def solution(mesh):
    in_specs = (P(None, "src"), P(None, "tgt"), P("src"), P("tgt"))
    out_specs = (P("src"), P("tgt"), P("src"), P(None, "src"), P(None, "tgt"))
    return jax.shard_map(
        per_device, mesh=mesh, in_specs=in_specs, out_specs=out_specs, check_vma=False
    )
```

```python
import math

import jax
import jax.numpy as jnp
from jax import lax
from jax.experimental import pallas as pl
from jax.experimental.pallas import tpu as pltpu
from jax.sharding import PartitionSpec as P

EPSILON = 0.1
LOG2E = math.log2(math.e)
KAPPA = LOG2E / EPSILON
LANES = 128
CHUNK = 256
LSE_CHUNK = 64
DEPTH = 64
HALF = 8
INNER = 8
FIRST = 5
STRIDE = 3
SAFE = 2.0**-80


def pieces(value):
    high = value.astype(jnp.bfloat16).astype(jnp.float32)
    rest = value - high
    mid = rest.astype(jnp.bfloat16).astype(jnp.float32)
    low = (rest - mid).astype(jnp.bfloat16).astype(jnp.float32)
    return high, mid, low


def tail_rows(count, dual, dual_first):
    row = lax.broadcasted_iota(jnp.int32, (16, count), 0)
    high, mid, low = pieces(dual)
    at = 0 if dual_first else 3
    ones_at = 3 - at
    out = jnp.where((row >= ones_at) & (row < ones_at + 3), 1.0, 0.0)
    out = jnp.where(row == at, high, out)
    out = jnp.where(row == at + 1, mid, out)
    return jnp.where(row == at + 2, low, out)


def fill_operands(a_points, a_dual, b_points, b_dual, a_ref, b_ref):
    features = a_points.shape[0]
    a = a_points.astype(jnp.float32)
    cross = 2.0 * KAPPA / features
    rows = jnp.concatenate([a, a, a, tail_rows(a.shape[1], a_dual, False)], axis=0)
    a_ref[...] = rows.T.astype(jnp.bfloat16)
    high, mid, low = pieces(b_points.astype(jnp.float32) * cross)
    b_ref[...] = jnp.concatenate(
        [high, mid, low, tail_rows(high.shape[1], b_dual, True)], axis=0
    ).astype(jnp.bfloat16)


def score_chunk(a_ref, b_ref, at, count):
    return jnp.dot(a_ref[at : at + count, :], b_ref[...], preferred_element_type=jnp.float32)


def by_sublane(array):
    return array.reshape(array.shape[0] // 8, 8, array.shape[1])


def lse_columns(a_ref, b_ref, b_dual, out_ref):
    def store(lse):
        for d in range(out_ref.shape[0]):
            out_ref[d] = lse - b_dual

    total = total_of(a_ref, b_ref)
    store(jnp.log(total) * LOG2E)

    @pl.when(jnp.min(total) < SAFE)
    def with_peaks():
        store(lse_of(a_ref, b_ref))


def lse_of(a_ref, b_ref):
    peak = None
    for at in range(0, a_ref.shape[0], LSE_CHUNK):
        scores = by_sublane(score_chunk(a_ref, b_ref, at, LSE_CHUNK))
        here = jnp.max(scores, axis=0)
        if peak is None:
            peak = here
            total = jnp.sum(jnp.exp2(scores - peak[None]), axis=0)
        else:
            risen = jnp.maximum(peak, here)
            total = total * jnp.exp2(peak - risen) + jnp.sum(
                jnp.exp2(scores - risen[None]), axis=0
            )
            peak = risen
    top = jnp.max(peak, axis=0, keepdims=True)
    total = jnp.sum(total * jnp.exp2(peak - top), axis=0, keepdims=True)
    return top + jnp.log(total) * LOG2E


def total_of(a_ref, b_ref):
    total = jnp.zeros((8, b_ref.shape[1]), jnp.float32)
    for at in range(0, a_ref.shape[0], CHUNK):
        total = total + jnp.sum(by_sublane(jnp.exp2(score_chunk(a_ref, b_ref, at, CHUNK))), axis=0)
    return jnp.sum(total, axis=0, keepdims=True)


def sum_columns(a_ref, b_ref, out_ref):
    total = total_of(a_ref, b_ref)
    for d in range(out_ref.shape[0]):
        out_ref[d] = total


def weighted_columns(a_ref, b_ref, points_ref, out_ref, split):
    features = points_ref.shape[0]
    share = features // split
    cols = b_ref.shape[1]
    total = jnp.zeros((8, cols), jnp.float32)
    moved = jnp.zeros((features, cols), jnp.float32)
    for at in range(0, a_ref.shape[0], CHUNK):
        weight = jnp.exp2(score_chunk(a_ref, b_ref, at, CHUNK))
        total = total + jnp.sum(by_sublane(weight), axis=0)
        points = points_ref[:, at : at + CHUNK]
        rounded = weight.astype(jnp.bfloat16)
        moved = moved + jnp.dot(points, rounded, preferred_element_type=jnp.float32)
    total = jnp.sum(total, axis=0, keepdims=True)
    for q in range(cols // LANES):
        lanes = slice(q * LANES, (q + 1) * LANES)
        for h in range(split):
            d = q * split + h
            out_ref[d, :, 0:LANES] = total[:, lanes]
            for k in range(share):
                out_ref[d, :, (k + 1) * LANES : (k + 2) * LANES] = moved[
                    h * share + k : h * share + k + 1, lanes
                ]


def norm_of(points_ref):
    points = points_ref[...].astype(jnp.float32)
    return jnp.sum(points * points, axis=0, keepdims=True)


def joined_lse(got_ref):
    parts = [got_ref[d] for d in range(got_ref.shape[0])]
    top = parts[0]
    for part in parts[1:]:
        top = jnp.maximum(top, part)
    total = jnp.exp2(parts[0] - top)
    for part in parts[1:]:
        total = total + jnp.exp2(part - top)
    return top + jnp.log(total) * LOG2E


def joined_sum(got_ref):
    total = got_ref[0]
    for d in range(1, got_ref.shape[0]):
        total = total + got_ref[d]
    return total


def log2_weight(logw_ref, whole):
    return (logw_ref[...] - math.log(whole)) * LOG2E


def clouds(xt_ref):
    features = xt_ref.shape[0] // 2
    return xt_ref.at[:features], xt_ref.at[features:]


def norm_dual(points_ref):
    return norm_of(points_ref) * (-KAPPA / points_ref.shape[0])


def first_rows(xt_ref, out_ref, a_ref, b_ref):
    x_ref, t_ref = clouds(xt_ref)
    over = norm_dual(x_ref)
    fill_operands(t_ref[...], norm_dual(t_ref), x_ref[...], over, a_ref, b_ref)
    lse_columns(a_ref, b_ref, over, out_ref)


def first_cols(whole, xt_ref, logw_ref, got_ref, alpha_ref, out_ref, a_ref, b_ref):
    x_ref, t_ref = clouds(xt_ref)
    alpha = log2_weight(logw_ref, whole) - joined_lse(got_ref)
    alpha_ref[...] = alpha
    over = norm_dual(t_ref)
    fill_operands(x_ref[...], alpha, t_ref[...], over, a_ref, b_ref)
    lse_columns(a_ref, b_ref, over, out_ref)


def second_rows(
    whole_s, whole_t, xt_ref, slogw_ref, tlogw_ref, alpha_ref, got_ref, beta_ref, out_ref, a_ref, b_ref
):
    x_ref, t_ref = clouds(xt_ref)
    beta = log2_weight(tlogw_ref, whole_t) - joined_lse(got_ref)
    beta_ref[...] = beta
    over = alpha_ref[...] - log2_weight(slogw_ref, whole_s)
    fill_operands(t_ref[...], beta, x_ref[...], over, a_ref, b_ref)
    sum_columns(a_ref, b_ref, out_ref)


def second_cols(
    whole_t, xt_ref, tlogw_ref, alpha_ref, beta_ref, got_ref, alpha2_ref, out_ref, a_ref, b_ref
):
    x_ref, t_ref = clouds(xt_ref)
    alpha = alpha_ref[...] - jnp.log(joined_sum(got_ref)) * LOG2E
    alpha2_ref[...] = alpha
    over = beta_ref[...] - log2_weight(tlogw_ref, whole_t)
    fill_operands(x_ref[...], alpha, t_ref[...], over, a_ref, b_ref)
    weighted_columns(a_ref, b_ref, x_ref, out_ref, x_ref.shape[0] // HALF)


def share_means(got_ref, out_ref):
    total = joined_sum(got_ref)
    mass = total[:, :LANES]
    for d in range(out_ref.shape[0]):
        out_ref[d, :, 0:LANES] = mass
    for at in range(LANES, total.shape[1], LANES):
        mean = total[:, at : at + LANES] / mass
        for d in range(out_ref.shape[0]):
            out_ref[d, :, at : at + LANES] = mean


def unpack_means(got_ref, means_ref, split):
    features = means_ref.shape[0]
    share = features // split
    masses = []
    for d in range(got_ref.shape[0]):
        q, h = divmod(d, split)
        if h == 0:
            masses.append(got_ref[d, :, 0:LANES])
        for k in range(share):
            means_ref[h * share + k : h * share + k + 1, q * LANES : (q + 1) * LANES] = got_ref[
                d, :, (k + 1) * LANES : (k + 2) * LANES
            ]
    return jnp.concatenate(masses, axis=1)


def last_rows(
    xt_ref, alpha_ref, beta_ref, got_ref, pulled_ref, pot_tgt_ref, out_ref, a_ref, b_ref
):
    x_ref, t_ref = clouds(xt_ref)
    mass = unpack_means(got_ref, pulled_ref, x_ref.shape[0] // HALF)
    beta = beta_ref[...] - jnp.log(mass) * LOG2E
    pot_tgt_ref[...] = beta * (1.0 / KAPPA) + norm_of(t_ref) * (1.0 / t_ref.shape[0])
    fill_operands(t_ref[...], beta, x_ref[...], alpha_ref[...], a_ref, b_ref)
    weighted_columns(a_ref, b_ref, t_ref, out_ref, 1)


def finish_rows(whole, xt_ref, logw_ref, alpha_ref, got_ref, projected_ref, ratio_ref, pot_src_ref):
    x_ref, _ = clouds(xt_ref)
    mass = unpack_means(got_ref, projected_ref, 1)
    ratio_ref[...] = mass * jnp.exp(math.log(whole) - logw_ref[...]) - 1.0
    pot_src_ref[...] = alpha_ref[...] * (1.0 / KAPPA) + norm_of(x_ref) * (1.0 / x_ref.shape[0])


def call(body, outs, *args, operands=None):
    scratch = []
    if operands is not None:
        scratch = [
            pltpu.VMEM((operands[0], DEPTH), jnp.bfloat16),
            pltpu.VMEM((DEPTH, operands[1]), jnp.bfloat16),
        ]
    return pl.pallas_call(
        body,
        out_shape=[jax.ShapeDtypeStruct(shape, jnp.float32) for shape in outs],
        scratch_shapes=scratch,
        compiler_params=pltpu.CompilerParams(vmem_limit_bytes=48 * 1024 * 1024),
    )(*args)


def spread(parts, axis, order):
    return lax.all_to_all(parts, axis, 0, 0, axis_index_groups=[order], tiled=True)


def per_device(x, t, source_logw, target_logw):
    features, rows = x.shape
    cols = t.shape[1]
    n_src, n_tgt = lax.axis_size("src"), lax.axis_size("tgt")
    whole_s, whole_t = rows * n_src, cols * n_tgt
    slogw = source_logw.reshape(1, rows)
    tlogw = target_logw.reshape(1, cols)
    split = features // HALF
    xt = jnp.concatenate([x, t], axis=0)
    outer = n_src // INNER
    by_src = [(r + outer // 2) % outer * INNER + (r // outer + FIRST) % INNER for r in range(n_src)]
    by_tgt = [(STRIDE * r + n_tgt // 2) % n_tgt for r in range(n_tgt)]
    assert rows == cols and n_src * LANES == cols * split and n_tgt * LANES == rows
    col_row = (n_src, 1, (HALF + 1) * LANES)
    row_row = (n_tgt, 1, (features + 1) * LANES)
    by_row, by_col = (cols, rows), (rows, cols)

    (lse,) = call(first_rows, [(n_tgt, 1, rows)], xt, operands=by_row)
    got = spread(lse, "tgt", by_tgt)

    def body(*refs):
        first_cols(whole_s, *refs)

    alpha, lse = call(body, [(1, rows), (n_src, 1, cols)], xt, slogw, got, operands=by_col)
    got = spread(lse, "src", by_src)

    def body(*refs):
        second_rows(whole_s, whole_t, *refs)

    beta, mass = call(
        body, [(1, cols), (n_tgt, 1, rows)], xt, slogw, tlogw, alpha, got, operands=by_row
    )
    got = spread(mass, "tgt", by_tgt)

    def body(*refs):
        second_cols(whole_t, *refs)

    alpha, sums = call(
        body, [(1, rows), col_row], xt, tlogw, alpha, beta, got, operands=by_col
    )
    got = spread(sums, "src", by_src)
    (means,) = call(share_means, [col_row], got)
    got = spread(means, "src", by_src)
    pulled, pot_tgt, sums = call(
        last_rows, [(features, cols), (1, cols), row_row], xt, alpha, beta, got, operands=by_row
    )
    got = spread(sums, "tgt", by_tgt)
    (means,) = call(share_means, [row_row], got)
    got = spread(means, "tgt", by_tgt)

    def body(*refs):
        finish_rows(whole_s, *refs)

    projected, ratio, pot_src = call(
        body, [(features, rows), (1, rows), (1, rows)], xt, slogw, alpha, got
    )
    return (pot_src.reshape(rows), pot_tgt.reshape(cols), ratio.reshape(rows), projected, pulled)


def solution(mesh):
    in_specs = (P(None, "src"), P(None, "tgt"), P("src"), P("tgt"))
    out_specs = (P("src"), P("tgt"), P("src"), P(None, "src"), P(None, "tgt"))
    return jax.shard_map(
        per_device, mesh=mesh, in_specs=in_specs, out_specs=out_specs, check_vma=False
    )
```

```python
import math

import jax
import jax.numpy as jnp
from jax import lax
from jax.experimental import pallas as pl
from jax.experimental.pallas import tpu as pltpu
from jax.sharding import PartitionSpec as P

EPSILON = 0.1
LOG2E = math.log2(math.e)
KAPPA = LOG2E / EPSILON
LANES = 128
CHUNK = 256
LSE_CHUNK = 64
DEPTH = 64
HALF = 8
INNER = 8
FIRST = 5
STRIDE = 3
SAFE = 2.0**-80


def pieces(value):
    high = value.astype(jnp.bfloat16).astype(jnp.float32)
    rest = value - high
    mid = rest.astype(jnp.bfloat16).astype(jnp.float32)
    low = (rest - mid).astype(jnp.bfloat16).astype(jnp.float32)
    return high, mid, low


def tail_rows(count, dual, dual_first):
    row = lax.broadcasted_iota(jnp.int32, (16, count), 0)
    high, mid, low = pieces(dual)
    at = 0 if dual_first else 3
    ones_at = 3 - at
    out = jnp.where((row >= ones_at) & (row < ones_at + 3), 1.0, 0.0)
    out = jnp.where(row == at, high, out)
    out = jnp.where(row == at + 1, mid, out)
    return jnp.where(row == at + 2, low, out)


def fill_operands(a_points, a_dual, b_points, b_dual, a_ref, b_ref):
    features = a_points.shape[0]
    a = a_points.astype(jnp.float32)
    cross = 2.0 * KAPPA / features
    rows = jnp.concatenate([a, a, a, tail_rows(a.shape[1], a_dual, False)], axis=0)
    a_ref[...] = rows.T.astype(jnp.bfloat16)
    high, mid, low = pieces(b_points.astype(jnp.float32) * cross)
    b_ref[...] = jnp.concatenate(
        [high, mid, low, tail_rows(high.shape[1], b_dual, True)], axis=0
    ).astype(jnp.bfloat16)


def score_chunk(a_ref, b_ref, at, count):
    return jnp.dot(a_ref[at : at + count, :], b_ref[...], preferred_element_type=jnp.float32)


def pack(row):
    width = row.shape[1] // 8
    return jnp.concatenate([row[:, r * width : (r + 1) * width] for r in range(8)], axis=0)


def unpack(tile):
    return jnp.concatenate([tile[r : r + 1, :] for r in range(8)], axis=1)


def by_sublane(array):
    return array.reshape(array.shape[0] // 8, 8, array.shape[1])


def lse_columns(a_ref, b_ref, b_dual, out_ref):
    def store(lse):
        for d in range(out_ref.shape[0]):
            out_ref[d] = lse - pack(b_dual)

    total = pack(total_of(a_ref, b_ref))
    store(jnp.log(total) * LOG2E)

    @pl.when(jnp.min(total) < SAFE)
    def with_peaks():
        store(pack(lse_of(a_ref, b_ref)))


def lse_of(a_ref, b_ref):
    peak = None
    for at in range(0, a_ref.shape[0], LSE_CHUNK):
        scores = by_sublane(score_chunk(a_ref, b_ref, at, LSE_CHUNK))
        here = jnp.max(scores, axis=0)
        if peak is None:
            peak = here
            total = jnp.sum(jnp.exp2(scores - peak[None]), axis=0)
        else:
            risen = jnp.maximum(peak, here)
            total = total * jnp.exp2(peak - risen) + jnp.sum(
                jnp.exp2(scores - risen[None]), axis=0
            )
            peak = risen
    top = jnp.max(peak, axis=0, keepdims=True)
    total = jnp.sum(total * jnp.exp2(peak - top), axis=0, keepdims=True)
    return top + jnp.log(total) * LOG2E


def total_of(a_ref, b_ref):
    total = jnp.zeros((8, b_ref.shape[1]), jnp.float32)
    for at in range(0, a_ref.shape[0], CHUNK):
        total = total + jnp.sum(by_sublane(jnp.exp2(score_chunk(a_ref, b_ref, at, CHUNK))), axis=0)
    return jnp.sum(total, axis=0, keepdims=True)


def sum_columns(a_ref, b_ref, out_ref):
    total = pack(total_of(a_ref, b_ref))
    for d in range(out_ref.shape[0]):
        out_ref[d] = total


def weighted_columns(a_ref, b_ref, points_ref, out_ref, split):
    features = points_ref.shape[0]
    share = features // split
    cols = b_ref.shape[1]
    total = jnp.zeros((8, cols), jnp.float32)
    moved = jnp.zeros((features, cols), jnp.float32)
    for at in range(0, a_ref.shape[0], CHUNK):
        weight = jnp.exp2(score_chunk(a_ref, b_ref, at, CHUNK))
        total = total + jnp.sum(by_sublane(weight), axis=0)
        points = points_ref[:, at : at + CHUNK]
        rounded = weight.astype(jnp.bfloat16)
        moved = moved + jnp.dot(points, rounded, preferred_element_type=jnp.float32)
    total = jnp.sum(total, axis=0, keepdims=True)
    for q in range(cols // LANES):
        lanes = slice(q * LANES, (q + 1) * LANES)
        for h in range(split):
            d = q * split + h
            out_ref[d, :, 0:LANES] = total[:, lanes]
            for k in range(share):
                out_ref[d, :, (k + 1) * LANES : (k + 2) * LANES] = moved[
                    h * share + k : h * share + k + 1, lanes
                ]


def norm_of(points_ref):
    points = points_ref[...].astype(jnp.float32)
    return jnp.sum(points * points, axis=0, keepdims=True)


def joined_lse(got_ref):
    parts = [got_ref[d] for d in range(got_ref.shape[0])]
    top = parts[0]
    for part in parts[1:]:
        top = jnp.maximum(top, part)
    total = jnp.exp2(parts[0] - top)
    for part in parts[1:]:
        total = total + jnp.exp2(part - top)
    return top + jnp.log(total) * LOG2E


def joined_sum(got_ref):
    total = got_ref[0]
    for d in range(1, got_ref.shape[0]):
        total = total + got_ref[d]
    return total


def log2_weight(logw_ref, whole):
    return (logw_ref[...] - math.log(whole)) * LOG2E


def clouds(xt_ref):
    features = xt_ref.shape[0] // 2
    return xt_ref.at[:features], xt_ref.at[features:]


def norm_dual(points_ref):
    return norm_of(points_ref) * (-KAPPA / points_ref.shape[0])


def first_rows(xt_ref, out_ref, a_ref, b_ref):
    x_ref, t_ref = clouds(xt_ref)
    over = norm_dual(x_ref)
    fill_operands(t_ref[...], norm_dual(t_ref), x_ref[...], over, a_ref, b_ref)
    lse_columns(a_ref, b_ref, over, out_ref)


def first_cols(whole, xt_ref, logw_ref, got_ref, alpha_ref, out_ref, a_ref, b_ref):
    x_ref, t_ref = clouds(xt_ref)
    alpha = log2_weight(logw_ref, whole) - unpack(joined_lse(got_ref))
    alpha_ref[...] = alpha
    over = norm_dual(t_ref)
    fill_operands(x_ref[...], alpha, t_ref[...], over, a_ref, b_ref)
    lse_columns(a_ref, b_ref, over, out_ref)


def second_rows(
    whole_s, whole_t, xt_ref, slogw_ref, tlogw_ref, alpha_ref, got_ref, beta_ref, out_ref, a_ref, b_ref
):
    x_ref, t_ref = clouds(xt_ref)
    beta = log2_weight(tlogw_ref, whole_t) - unpack(joined_lse(got_ref))
    beta_ref[...] = beta
    over = alpha_ref[...] - log2_weight(slogw_ref, whole_s)
    fill_operands(t_ref[...], beta, x_ref[...], over, a_ref, b_ref)
    sum_columns(a_ref, b_ref, out_ref)


def second_cols(
    whole_t, xt_ref, tlogw_ref, alpha_ref, beta_ref, got_ref, alpha2_ref, out_ref, a_ref, b_ref
):
    x_ref, t_ref = clouds(xt_ref)
    alpha = alpha_ref[...] - unpack(jnp.log(joined_sum(got_ref)) * LOG2E)
    alpha2_ref[...] = alpha
    over = beta_ref[...] - log2_weight(tlogw_ref, whole_t)
    fill_operands(x_ref[...], alpha, t_ref[...], over, a_ref, b_ref)
    weighted_columns(a_ref, b_ref, x_ref, out_ref, x_ref.shape[0] // HALF)


def share_means(got_ref, out_ref):
    total = joined_sum(got_ref)
    mass = total[:, :LANES]
    for d in range(out_ref.shape[0]):
        out_ref[d, :, 0:LANES] = mass
    for at in range(LANES, total.shape[1], LANES):
        mean = total[:, at : at + LANES] / mass
        for d in range(out_ref.shape[0]):
            out_ref[d, :, at : at + LANES] = mean


def unpack_means(got_ref, means_ref, split):
    features = means_ref.shape[0]
    share = features // split
    masses = []
    for d in range(got_ref.shape[0]):
        q, h = divmod(d, split)
        if h == 0:
            masses.append(got_ref[d, :, 0:LANES])
        for k in range(share):
            means_ref[h * share + k : h * share + k + 1, q * LANES : (q + 1) * LANES] = got_ref[
                d, :, (k + 1) * LANES : (k + 2) * LANES
            ]
    return jnp.concatenate(masses, axis=1)


def last_rows(
    xt_ref, alpha_ref, beta_ref, got_ref, means_ref, beta2_ref, out_ref, a_ref, b_ref
):
    x_ref, t_ref = clouds(xt_ref)
    mass = unpack_means(got_ref, means_ref, x_ref.shape[0] // HALF)
    beta = beta_ref[...] - jnp.log(mass) * LOG2E
    beta2_ref[...] = beta
    fill_operands(t_ref[...], beta, x_ref[...], alpha_ref[...], a_ref, b_ref)
    weighted_columns(a_ref, b_ref, t_ref, out_ref, 1)


def finish_rows(
    whole,
    xt_ref,
    logw_ref,
    alpha_ref,
    beta_ref,
    means_ref,
    got_ref,
    projected_ref,
    ratio_ref,
    pot_src_ref,
    pulled_ref,
    pot_tgt_ref,
):
    x_ref, t_ref = clouds(xt_ref)
    pulled_ref[...] = means_ref[...]
    pot_tgt_ref[...] = beta_ref[...] * (1.0 / KAPPA) + norm_of(t_ref) * (1.0 / t_ref.shape[0])
    mass = unpack_means(got_ref, projected_ref, 1)
    ratio_ref[...] = mass * jnp.exp(math.log(whole) - logw_ref[...]) - 1.0
    pot_src_ref[...] = alpha_ref[...] * (1.0 / KAPPA) + norm_of(x_ref) * (1.0 / x_ref.shape[0])


def call(body, outs, *args, operands=None):
    scratch = []
    if operands is not None:
        scratch = [
            pltpu.VMEM((operands[0], DEPTH), jnp.bfloat16),
            pltpu.VMEM((DEPTH, operands[1]), jnp.bfloat16),
        ]
    return pl.pallas_call(
        body,
        out_shape=[jax.ShapeDtypeStruct(shape, jnp.float32) for shape in outs],
        scratch_shapes=scratch,
        compiler_params=pltpu.CompilerParams(vmem_limit_bytes=48 * 1024 * 1024),
    )(*args)


def spread(parts, axis, order):
    return lax.all_to_all(parts, axis, 0, 0, axis_index_groups=[order], tiled=True)


def per_device(x, t, source_logw, target_logw):
    features, rows = x.shape
    cols = t.shape[1]
    n_src, n_tgt = lax.axis_size("src"), lax.axis_size("tgt")
    whole_s, whole_t = rows * n_src, cols * n_tgt
    slogw = source_logw.reshape(1, rows)
    tlogw = target_logw.reshape(1, cols)
    split = features // HALF
    xt = jnp.concatenate([x, t], axis=0)
    outer = n_src // INNER
    by_src = [(r + outer // 2) % outer * INNER + (r // outer + FIRST) % INNER for r in range(n_src)]
    by_tgt = [(STRIDE * r + n_tgt // 2) % n_tgt for r in range(n_tgt)]
    assert rows == cols and n_src * LANES == cols * split and n_tgt * LANES == rows
    col_row = (n_src, 1, (HALF + 1) * LANES)
    row_row = (n_tgt, 1, (features + 1) * LANES)
    by_row, by_col = (cols, rows), (rows, cols)

    (lse,) = call(first_rows, [(n_tgt, 8, rows // 8)], xt, operands=by_row)
    got = spread(lse, "tgt", by_tgt)

    def body(*refs):
        first_cols(whole_s, *refs)

    alpha, lse = call(body, [(1, rows), (n_src, 8, cols // 8)], xt, slogw, got, operands=by_col)
    got = spread(lse, "src", by_src)

    def body(*refs):
        second_rows(whole_s, whole_t, *refs)

    beta, mass = call(
        body, [(1, cols), (n_tgt, 8, rows // 8)], xt, slogw, tlogw, alpha, got, operands=by_row
    )
    got = spread(mass, "tgt", by_tgt)

    def body(*refs):
        second_cols(whole_t, *refs)

    alpha, sums = call(
        body, [(1, rows), col_row], xt, tlogw, alpha, beta, got, operands=by_col
    )
    got = spread(sums, "src", by_src)
    (means,) = call(share_means, [col_row], got)
    got = spread(means, "src", by_src)
    target_means, beta, sums = call(
        last_rows, [(features, cols), (1, cols), row_row], xt, alpha, beta, got, operands=by_row
    )
    got = spread(sums, "tgt", by_tgt)
    (means,) = call(share_means, [row_row], got)
    got = spread(means, "tgt", by_tgt)

    def body(*refs):
        finish_rows(whole_s, *refs)

    projected, ratio, pot_src, pulled, pot_tgt = call(
        body,
        [(features, rows), (1, rows), (1, rows), (features, cols), (1, cols)],
        xt,
        slogw,
        alpha,
        beta,
        target_means,
        got,
    )
    return (pot_src.reshape(rows), pot_tgt.reshape(cols), ratio.reshape(rows), projected, pulled)


def solution(mesh):
    in_specs = (P(None, "src"), P(None, "tgt"), P("src"), P("tgt"))
    out_specs = (P("src"), P("tgt"), P("src"), P(None, "src"), P(None, "tgt"))
    return jax.shard_map(
        per_device, mesh=mesh, in_specs=in_specs, out_specs=out_specs, check_vma=False
    )
```

```python
import math

import jax
import jax.numpy as jnp
from jax import lax
from jax.experimental import pallas as pl
from jax.experimental.pallas import tpu as pltpu
from jax.sharding import PartitionSpec as P

EPSILON = 0.1
LOG2E = math.log2(math.e)
KAPPA = LOG2E / EPSILON
LANES = 128
CHUNK = 512
LSE_CHUNK = 64
DEPTH = 64
HALF = 8
INNER = 8
FIRST = 5
STRIDE = 3
SAFE = 2.0**-80


def pieces(value):
    high = value.astype(jnp.bfloat16).astype(jnp.float32)
    rest = value - high
    mid = rest.astype(jnp.bfloat16).astype(jnp.float32)
    low = (rest - mid).astype(jnp.bfloat16).astype(jnp.float32)
    return high, mid, low


def tail_rows(count, dual, dual_first):
    row = lax.broadcasted_iota(jnp.int32, (16, count), 0)
    high, mid, low = pieces(dual)
    at = 0 if dual_first else 3
    ones_at = 3 - at
    out = jnp.where((row >= ones_at) & (row < ones_at + 3), 1.0, 0.0)
    out = jnp.where(row == at, high, out)
    out = jnp.where(row == at + 1, mid, out)
    return jnp.where(row == at + 2, low, out)


def fill_operands(a_points, a_dual, b_points, b_dual, a_ref, b_ref):
    features = a_points.shape[0]
    a = a_points.astype(jnp.float32)
    cross = 2.0 * KAPPA / features
    rows = jnp.concatenate([a, a, a, tail_rows(a.shape[1], a_dual, False)], axis=0)
    a_ref[...] = rows.T.astype(jnp.bfloat16)
    high, mid, low = pieces(b_points.astype(jnp.float32) * cross)
    b_ref[...] = jnp.concatenate(
        [high, mid, low, tail_rows(high.shape[1], b_dual, True)], axis=0
    ).astype(jnp.bfloat16)


def score_chunk(a_ref, b_ref, at, count):
    return jnp.dot(a_ref[at : at + count, :], b_ref[...], preferred_element_type=jnp.float32)


def pack(row):
    width = row.shape[1] // 8
    return jnp.concatenate([row[:, r * width : (r + 1) * width] for r in range(8)], axis=0)


def unpack(tile):
    return jnp.concatenate([tile[r : r + 1, :] for r in range(8)], axis=1)


def by_sublane(array):
    return array.reshape(array.shape[0] // 8, 8, array.shape[1])


def lse_columns(a_ref, b_ref, b_dual, out_ref):
    def store(lse):
        for d in range(out_ref.shape[0]):
            out_ref[d] = lse - pack(b_dual)

    total = pack(total_of(a_ref, b_ref))
    store(jnp.log(total) * LOG2E)

    @pl.when(jnp.min(total) < SAFE)
    def with_peaks():
        store(pack(lse_of(a_ref, b_ref)))


def lse_of(a_ref, b_ref):
    peak = None
    for at in range(0, a_ref.shape[0], LSE_CHUNK):
        scores = by_sublane(score_chunk(a_ref, b_ref, at, LSE_CHUNK))
        here = jnp.max(scores, axis=0)
        if peak is None:
            peak = here
            total = jnp.sum(jnp.exp2(scores - peak[None]), axis=0)
        else:
            risen = jnp.maximum(peak, here)
            total = total * jnp.exp2(peak - risen) + jnp.sum(
                jnp.exp2(scores - risen[None]), axis=0
            )
            peak = risen
    top = jnp.max(peak, axis=0, keepdims=True)
    total = jnp.sum(total * jnp.exp2(peak - top), axis=0, keepdims=True)
    return top + jnp.log(total) * LOG2E


def total_of(a_ref, b_ref):
    total = jnp.zeros((8, b_ref.shape[1]), jnp.float32)
    for at in range(0, a_ref.shape[0], CHUNK):
        total = total + jnp.sum(by_sublane(jnp.exp2(score_chunk(a_ref, b_ref, at, CHUNK))), axis=0)
    return jnp.sum(total, axis=0, keepdims=True)


def sum_columns(a_ref, b_ref, out_ref):
    total = pack(total_of(a_ref, b_ref))
    for d in range(out_ref.shape[0]):
        out_ref[d] = total


def weighted_columns(a_ref, b_ref, points_ref, out_ref, split):
    features = points_ref.shape[0]
    share = features // split
    cols = b_ref.shape[1]
    total = jnp.zeros((8, cols), jnp.float32)
    moved = jnp.zeros((features, cols), jnp.float32)
    for at in range(0, a_ref.shape[0], CHUNK):
        weight = jnp.exp2(score_chunk(a_ref, b_ref, at, CHUNK))
        total = total + jnp.sum(by_sublane(weight), axis=0)
        points = points_ref[:, at : at + CHUNK]
        rounded = weight.astype(jnp.bfloat16)
        moved = moved + jnp.dot(points, rounded, preferred_element_type=jnp.float32)
    total = jnp.sum(total, axis=0, keepdims=True)
    for q in range(cols // LANES):
        lanes = slice(q * LANES, (q + 1) * LANES)
        for h in range(split):
            d = q * split + h
            out_ref[d, :, 0:LANES] = total[:, lanes]
            for k in range(share):
                out_ref[d, :, (k + 1) * LANES : (k + 2) * LANES] = moved[
                    h * share + k : h * share + k + 1, lanes
                ]


def norm_of(points_ref):
    points = points_ref[...].astype(jnp.float32)
    return jnp.sum(points * points, axis=0, keepdims=True)


def joined_lse(got_ref):
    parts = [got_ref[d] for d in range(got_ref.shape[0])]
    top = parts[0]
    for part in parts[1:]:
        top = jnp.maximum(top, part)
    total = jnp.exp2(parts[0] - top)
    for part in parts[1:]:
        total = total + jnp.exp2(part - top)
    return top + jnp.log(total) * LOG2E


def joined_sum(got_ref):
    total = got_ref[0]
    for d in range(1, got_ref.shape[0]):
        total = total + got_ref[d]
    return total


def log2_weight(logw_ref, whole):
    return (logw_ref[...] - math.log(whole)) * LOG2E


def clouds(xt_ref):
    features = xt_ref.shape[0] // 2
    return xt_ref.at[:features], xt_ref.at[features:]


def norm_dual(points_ref):
    return norm_of(points_ref) * (-KAPPA / points_ref.shape[0])


def first_rows(xt_ref, out_ref, a_ref, b_ref):
    x_ref, t_ref = clouds(xt_ref)
    over = norm_dual(x_ref)
    fill_operands(t_ref[...], norm_dual(t_ref), x_ref[...], over, a_ref, b_ref)
    lse_columns(a_ref, b_ref, over, out_ref)


def first_cols(whole, xt_ref, logw_ref, got_ref, alpha_ref, out_ref, a_ref, b_ref):
    x_ref, t_ref = clouds(xt_ref)
    alpha = log2_weight(logw_ref, whole) - unpack(joined_lse(got_ref))
    alpha_ref[...] = alpha
    over = norm_dual(t_ref)
    fill_operands(x_ref[...], alpha, t_ref[...], over, a_ref, b_ref)
    lse_columns(a_ref, b_ref, over, out_ref)


def second_rows(
    whole_s, whole_t, xt_ref, slogw_ref, tlogw_ref, alpha_ref, got_ref, beta_ref, out_ref, a_ref, b_ref
):
    x_ref, t_ref = clouds(xt_ref)
    beta = log2_weight(tlogw_ref, whole_t) - unpack(joined_lse(got_ref))
    beta_ref[...] = beta
    over = alpha_ref[...] - log2_weight(slogw_ref, whole_s)
    fill_operands(t_ref[...], beta, x_ref[...], over, a_ref, b_ref)
    sum_columns(a_ref, b_ref, out_ref)


def second_cols(
    whole_t, xt_ref, tlogw_ref, alpha_ref, beta_ref, got_ref, alpha2_ref, out_ref, a_ref, b_ref
):
    x_ref, t_ref = clouds(xt_ref)
    alpha = alpha_ref[...] - unpack(jnp.log(joined_sum(got_ref)) * LOG2E)
    alpha2_ref[...] = alpha
    over = beta_ref[...] - log2_weight(tlogw_ref, whole_t)
    fill_operands(x_ref[...], alpha, t_ref[...], over, a_ref, b_ref)
    weighted_columns(a_ref, b_ref, x_ref, out_ref, x_ref.shape[0] // HALF)


def share_means(got_ref, out_ref):
    total = joined_sum(got_ref)
    mass = total[:, :LANES]
    for d in range(out_ref.shape[0]):
        out_ref[d, :, 0:LANES] = mass
    for at in range(LANES, total.shape[1], LANES):
        mean = total[:, at : at + LANES] / mass
        for d in range(out_ref.shape[0]):
            out_ref[d, :, at : at + LANES] = mean


def unpack_means(got_ref, means_ref, split):
    features = means_ref.shape[0]
    share = features // split
    masses = []
    for d in range(got_ref.shape[0]):
        q, h = divmod(d, split)
        if h == 0:
            masses.append(got_ref[d, :, 0:LANES])
        for k in range(share):
            means_ref[h * share + k : h * share + k + 1, q * LANES : (q + 1) * LANES] = got_ref[
                d, :, (k + 1) * LANES : (k + 2) * LANES
            ]
    return jnp.concatenate(masses, axis=1)


def last_rows(
    xt_ref, alpha_ref, beta_ref, got_ref, means_ref, beta2_ref, out_ref, a_ref, b_ref
):
    x_ref, t_ref = clouds(xt_ref)
    mass = unpack_means(got_ref, means_ref, x_ref.shape[0] // HALF)
    beta = beta_ref[...] - jnp.log(mass) * LOG2E
    beta2_ref[...] = beta
    fill_operands(t_ref[...], beta, x_ref[...], alpha_ref[...], a_ref, b_ref)
    weighted_columns(a_ref, b_ref, t_ref, out_ref, 1)


def finish_rows(
    whole,
    xt_ref,
    logw_ref,
    alpha_ref,
    beta_ref,
    means_ref,
    got_ref,
    projected_ref,
    ratio_ref,
    pot_src_ref,
    pulled_ref,
    pot_tgt_ref,
):
    x_ref, t_ref = clouds(xt_ref)
    pulled_ref[...] = means_ref[...]
    pot_tgt_ref[...] = beta_ref[...] * (1.0 / KAPPA) + norm_of(t_ref) * (1.0 / t_ref.shape[0])
    mass = unpack_means(got_ref, projected_ref, 1)
    ratio_ref[...] = mass * jnp.exp(math.log(whole) - logw_ref[...]) - 1.0
    pot_src_ref[...] = alpha_ref[...] * (1.0 / KAPPA) + norm_of(x_ref) * (1.0 / x_ref.shape[0])


def call(body, outs, *args, operands=None):
    scratch = []
    if operands is not None:
        scratch = [
            pltpu.VMEM((operands[0], DEPTH), jnp.bfloat16),
            pltpu.VMEM((DEPTH, operands[1]), jnp.bfloat16),
        ]
    return pl.pallas_call(
        body,
        out_shape=[jax.ShapeDtypeStruct(shape, jnp.float32) for shape in outs],
        scratch_shapes=scratch,
        compiler_params=pltpu.CompilerParams(vmem_limit_bytes=48 * 1024 * 1024),
    )(*args)


def spread(parts, axis, groups):
    return lax.all_to_all(parts, axis, 0, 0, axis_index_groups=groups, tiled=True)


def per_device(x, t, source_logw, target_logw):
    features, rows = x.shape
    cols = t.shape[1]
    n_src, n_tgt = lax.axis_size("src"), lax.axis_size("tgt")
    whole_s, whole_t = rows * n_src, cols * n_tgt
    slogw = source_logw.reshape(1, rows)
    tlogw = target_logw.reshape(1, cols)
    split = features // HALF
    xt = jnp.concatenate([x, t], axis=0)
    outer = n_src // INNER
    one_src = [(r + outer // 2) % outer * INNER + (r // outer + FIRST) % INNER for r in range(n_src)]
    by_src = [
        [(one_src if t % 2 == 0 else one_src[:1] + one_src[:0:-1])[r] * n_tgt + t for r in range(n_src)]
        for t in range(n_tgt)
    ]
    by_tgt = [[(STRIDE * r + n_tgt // 2) % n_tgt for r in range(n_tgt)]]
    assert rows == cols and n_src * LANES == cols * split and n_tgt * LANES == rows
    col_row = (n_src, 1, (HALF + 1) * LANES)
    row_row = (n_tgt, 1, (features + 1) * LANES)
    by_row, by_col = (cols, rows), (rows, cols)

    (lse,) = call(first_rows, [(n_tgt, 8, rows // 8)], xt, operands=by_row)
    got = spread(lse, "tgt", by_tgt)

    def body(*refs):
        first_cols(whole_s, *refs)

    alpha, lse = call(body, [(1, rows), (n_src, 8, cols // 8)], xt, slogw, got, operands=by_col)
    got = spread(lse, ("src", "tgt"), by_src)

    def body(*refs):
        second_rows(whole_s, whole_t, *refs)

    beta, mass = call(
        body, [(1, cols), (n_tgt, 8, rows // 8)], xt, slogw, tlogw, alpha, got, operands=by_row
    )
    got = spread(mass, "tgt", by_tgt)

    def body(*refs):
        second_cols(whole_t, *refs)

    alpha, sums = call(
        body, [(1, rows), col_row], xt, tlogw, alpha, beta, got, operands=by_col
    )
    got = spread(sums, ("src", "tgt"), by_src)
    (means,) = call(share_means, [col_row], got)
    got = spread(means, ("src", "tgt"), by_src)
    target_means, beta, sums = call(
        last_rows, [(features, cols), (1, cols), row_row], xt, alpha, beta, got, operands=by_row
    )
    got = spread(sums, "tgt", by_tgt)
    (means,) = call(share_means, [row_row], got)
    got = spread(means, "tgt", by_tgt)

    def body(*refs):
        finish_rows(whole_s, *refs)

    projected, ratio, pot_src, pulled, pot_tgt = call(
        body,
        [(features, rows), (1, rows), (1, rows), (features, cols), (1, cols)],
        xt,
        slogw,
        alpha,
        beta,
        target_means,
        got,
    )
    return (pot_src.reshape(rows), pot_tgt.reshape(cols), ratio.reshape(rows), projected, pulled)


def solution(mesh):
    in_specs = (P(None, "src"), P(None, "tgt"), P("src"), P("tgt"))
    out_specs = (P("src"), P("tgt"), P("src"), P(None, "src"), P(None, "tgt"))
    return jax.shard_map(
        per_device, mesh=mesh, in_specs=in_specs, out_specs=out_specs, check_vma=False
    )
```

```python
import math

import jax
import jax.numpy as jnp
from jax import lax
from jax.experimental import pallas as pl
from jax.experimental.pallas import tpu as pltpu
from jax.sharding import PartitionSpec as P

EPSILON = 0.1
LOG2E = math.log2(math.e)
KAPPA = LOG2E / EPSILON
LANES = 128
CHUNK = 256
LSE_CHUNK = 64
WEIGHTED_CHUNK = 512
DEPTH = 64
HALF = 8
INNER = 8
FIRST = 4
STRIDE = 3
SAFE = 2.0**-80


def pieces(value):
    high = value.astype(jnp.bfloat16).astype(jnp.float32)
    rest = value - high
    mid = rest.astype(jnp.bfloat16).astype(jnp.float32)
    low = (rest - mid).astype(jnp.bfloat16).astype(jnp.float32)
    return high, mid, low


def tail_rows(count, dual, dual_first):
    row = lax.broadcasted_iota(jnp.int32, (16, count), 0)
    high, mid, low = pieces(dual)
    at = 0 if dual_first else 3
    ones_at = 3 - at
    out = jnp.where((row >= ones_at) & (row < ones_at + 3), 1.0, 0.0)
    out = jnp.where(row == at, high, out)
    out = jnp.where(row == at + 1, mid, out)
    return jnp.where(row == at + 2, low, out)


def fill_operands(a_points, a_dual, b_points, b_dual, a_ref, b_ref):
    features = a_points.shape[0]
    a = a_points.astype(jnp.float32)
    cross = 2.0 * KAPPA / features
    rows = jnp.concatenate([a, a, a, tail_rows(a.shape[1], a_dual, False)], axis=0)
    a_ref[...] = rows.T.astype(jnp.bfloat16)
    high, mid, low = pieces(b_points.astype(jnp.float32) * cross)
    b_ref[...] = jnp.concatenate(
        [high, mid, low, tail_rows(high.shape[1], b_dual, True)], axis=0
    ).astype(jnp.bfloat16)


def score_chunk(a_ref, b_ref, at, count):
    return jnp.dot(a_ref[at : at + count, :], b_ref[...], preferred_element_type=jnp.float32)


def pack(row):
    width = row.shape[1] // 8
    return jnp.concatenate([row[:, r * width : (r + 1) * width] for r in range(8)], axis=0)


def unpack(tile):
    return jnp.concatenate([tile[r : r + 1, :] for r in range(8)], axis=1)


def by_sublane(array):
    return array.reshape(array.shape[0] // 8, 8, array.shape[1])


def lse_columns(a_ref, b_ref, b_dual, out_ref):
    def store(lse):
        for d in range(out_ref.shape[0]):
            out_ref[d] = lse - pack(b_dual)

    total = pack(total_of(a_ref, b_ref))
    store(jnp.log(total) * LOG2E)

    @pl.when(jnp.min(total) < SAFE)
    def with_peaks():
        store(pack(lse_of(a_ref, b_ref)))


def lse_of(a_ref, b_ref):
    peak = None
    for at in range(0, a_ref.shape[0], LSE_CHUNK):
        scores = by_sublane(score_chunk(a_ref, b_ref, at, LSE_CHUNK))
        here = jnp.max(scores, axis=0)
        if peak is None:
            peak = here
            total = jnp.sum(jnp.exp2(scores - peak[None]), axis=0)
        else:
            risen = jnp.maximum(peak, here)
            total = total * jnp.exp2(peak - risen) + jnp.sum(
                jnp.exp2(scores - risen[None]), axis=0
            )
            peak = risen
    top = jnp.max(peak, axis=0, keepdims=True)
    total = jnp.sum(total * jnp.exp2(peak - top), axis=0, keepdims=True)
    return top + jnp.log(total) * LOG2E


def total_of(a_ref, b_ref):
    total = jnp.zeros((8, b_ref.shape[1]), jnp.float32)
    for at in range(0, a_ref.shape[0], CHUNK):
        total = total + jnp.sum(by_sublane(jnp.exp2(score_chunk(a_ref, b_ref, at, CHUNK))), axis=0)
    return jnp.sum(total, axis=0, keepdims=True)


def sum_columns(a_ref, b_ref, out_ref):
    total = pack(total_of(a_ref, b_ref))
    for d in range(out_ref.shape[0]):
        out_ref[d] = total


def weighted_columns(a_ref, b_ref, points_ref, out_ref, split):
    features = points_ref.shape[0]
    share = features // split
    cols = b_ref.shape[1]
    total = jnp.zeros((8, cols), jnp.float32)
    moved = jnp.zeros((features, cols), jnp.float32)
    for at in range(0, a_ref.shape[0], WEIGHTED_CHUNK):
        weight = jnp.exp2(score_chunk(a_ref, b_ref, at, WEIGHTED_CHUNK))
        total = total + jnp.sum(by_sublane(weight), axis=0)
        points = points_ref[:, at : at + WEIGHTED_CHUNK]
        rounded = weight.astype(jnp.bfloat16)
        moved = moved + jnp.dot(points, rounded, preferred_element_type=jnp.float32)
    total = jnp.sum(total, axis=0, keepdims=True)
    for q in range(cols // LANES):
        lanes = slice(q * LANES, (q + 1) * LANES)
        for h in range(split):
            d = q * split + h
            out_ref[d, :, 0:LANES] = total[:, lanes]
            for k in range(share):
                out_ref[d, :, (k + 1) * LANES : (k + 2) * LANES] = moved[
                    h * share + k : h * share + k + 1, lanes
                ]


def norm_of(points_ref):
    points = points_ref[...].astype(jnp.float32)
    return jnp.sum(points * points, axis=0, keepdims=True)


def joined_lse(got_ref):
    parts = [got_ref[d] for d in range(got_ref.shape[0])]
    top = parts[0]
    for part in parts[1:]:
        top = jnp.maximum(top, part)
    total = jnp.exp2(parts[0] - top)
    for part in parts[1:]:
        total = total + jnp.exp2(part - top)
    return top + jnp.log(total) * LOG2E


def joined_sum(got_ref):
    total = got_ref[0]
    for d in range(1, got_ref.shape[0]):
        total = total + got_ref[d]
    return total


def log2_weight(logw_ref, whole):
    return (logw_ref[...] - math.log(whole)) * LOG2E


def clouds(xt_ref):
    features = xt_ref.shape[0] // 2
    return xt_ref.at[:features], xt_ref.at[features:]


def norm_dual(points_ref):
    return norm_of(points_ref) * (-KAPPA / points_ref.shape[0])


def first_rows(xt_ref, out_ref, a_ref, b_ref):
    x_ref, t_ref = clouds(xt_ref)
    over = norm_dual(x_ref)
    fill_operands(t_ref[...], norm_dual(t_ref), x_ref[...], over, a_ref, b_ref)
    lse_columns(a_ref, b_ref, over, out_ref)


def first_cols(whole, xt_ref, logw_ref, got_ref, alpha_ref, out_ref, a_ref, b_ref):
    x_ref, t_ref = clouds(xt_ref)
    alpha = log2_weight(logw_ref, whole) - unpack(joined_lse(got_ref))
    alpha_ref[...] = alpha
    over = norm_dual(t_ref)
    fill_operands(x_ref[...], alpha, t_ref[...], over, a_ref, b_ref)
    lse_columns(a_ref, b_ref, over, out_ref)


def second_rows(
    whole_s, whole_t, xt_ref, slogw_ref, tlogw_ref, alpha_ref, got_ref, beta_ref, out_ref, a_ref, b_ref
):
    x_ref, t_ref = clouds(xt_ref)
    beta = log2_weight(tlogw_ref, whole_t) - unpack(joined_lse(got_ref))
    beta_ref[...] = beta
    over = alpha_ref[...] - log2_weight(slogw_ref, whole_s)
    fill_operands(t_ref[...], beta, x_ref[...], over, a_ref, b_ref)
    sum_columns(a_ref, b_ref, out_ref)


def second_cols(
    whole_t, xt_ref, tlogw_ref, alpha_ref, beta_ref, got_ref, alpha2_ref, out_ref, a_ref, b_ref
):
    x_ref, t_ref = clouds(xt_ref)
    alpha = alpha_ref[...] - unpack(jnp.log(joined_sum(got_ref)) * LOG2E)
    alpha2_ref[...] = alpha
    over = beta_ref[...] - log2_weight(tlogw_ref, whole_t)
    fill_operands(x_ref[...], alpha, t_ref[...], over, a_ref, b_ref)
    weighted_columns(a_ref, b_ref, x_ref, out_ref, x_ref.shape[0] // HALF)


def share_means(got_ref, out_ref):
    total = joined_sum(got_ref)
    mass = total[:, :LANES]
    for d in range(out_ref.shape[0]):
        out_ref[d, :, 0:LANES] = mass
    for at in range(LANES, total.shape[1], LANES):
        mean = total[:, at : at + LANES] / mass
        for d in range(out_ref.shape[0]):
            out_ref[d, :, at : at + LANES] = mean


def unpack_means(got_ref, means_ref, split):
    features = means_ref.shape[0]
    share = features // split
    masses = []
    for d in range(got_ref.shape[0]):
        q, h = divmod(d, split)
        if h == 0:
            masses.append(got_ref[d, :, 0:LANES])
        for k in range(share):
            means_ref[h * share + k : h * share + k + 1, q * LANES : (q + 1) * LANES] = got_ref[
                d, :, (k + 1) * LANES : (k + 2) * LANES
            ]
    return jnp.concatenate(masses, axis=1)


def last_rows(
    xt_ref, alpha_ref, beta_ref, got_ref, means_ref, beta2_ref, out_ref, a_ref, b_ref
):
    x_ref, t_ref = clouds(xt_ref)
    mass = unpack_means(got_ref, means_ref, x_ref.shape[0] // HALF)
    beta = beta_ref[...] - jnp.log(mass) * LOG2E
    beta2_ref[...] = beta
    fill_operands(t_ref[...], beta, x_ref[...], alpha_ref[...], a_ref, b_ref)
    weighted_columns(a_ref, b_ref, t_ref, out_ref, 1)


def finish_rows(
    whole,
    xt_ref,
    logw_ref,
    alpha_ref,
    beta_ref,
    means_ref,
    got_ref,
    projected_ref,
    ratio_ref,
    pot_src_ref,
    pulled_ref,
    pot_tgt_ref,
):
    x_ref, t_ref = clouds(xt_ref)
    pulled_ref[...] = means_ref[...]
    pot_tgt_ref[...] = beta_ref[...] * (1.0 / KAPPA) + norm_of(t_ref) * (1.0 / t_ref.shape[0])
    mass = unpack_means(got_ref, projected_ref, 1)
    ratio_ref[...] = mass * jnp.exp(math.log(whole) - logw_ref[...]) - 1.0
    pot_src_ref[...] = alpha_ref[...] * (1.0 / KAPPA) + norm_of(x_ref) * (1.0 / x_ref.shape[0])


def call(body, outs, *args, operands=None):
    scratch = []
    if operands is not None:
        scratch = [
            pltpu.VMEM((operands[0], DEPTH), jnp.bfloat16),
            pltpu.VMEM((DEPTH, operands[1]), jnp.bfloat16),
        ]
    return pl.pallas_call(
        body,
        out_shape=[jax.ShapeDtypeStruct(shape, jnp.float32) for shape in outs],
        scratch_shapes=scratch,
        compiler_params=pltpu.CompilerParams(vmem_limit_bytes=48 * 1024 * 1024),
    )(*args)


def spread(parts, axis, order):
    return lax.all_to_all(parts, axis, 0, 0, axis_index_groups=[order], tiled=True)


def per_device(x, t, source_logw, target_logw):
    features, rows = x.shape
    cols = t.shape[1]
    n_src, n_tgt = lax.axis_size("src"), lax.axis_size("tgt")
    whole_s, whole_t = rows * n_src, cols * n_tgt
    slogw = source_logw.reshape(1, rows)
    tlogw = target_logw.reshape(1, cols)
    split = features // HALF
    xt = jnp.concatenate([x, t], axis=0)
    outer = n_src // INNER
    by_src = [(r + outer // 2) % outer * INNER + (r // outer + FIRST) % INNER for r in range(n_src)]
    by_tgt = [(STRIDE * r + n_tgt // 2) % n_tgt for r in range(n_tgt)]
    assert rows == cols and n_src * LANES == cols * split and n_tgt * LANES == rows
    col_row = (n_src, 1, (HALF + 1) * LANES)
    row_row = (n_tgt, 1, (features + 1) * LANES)
    by_row, by_col = (cols, rows), (rows, cols)

    (lse,) = call(first_rows, [(n_tgt, 8, rows // 8)], xt, operands=by_row)
    got = spread(lse, "tgt", by_tgt)

    def body(*refs):
        first_cols(whole_s, *refs)

    alpha, lse = call(body, [(1, rows), (n_src, 8, cols // 8)], xt, slogw, got, operands=by_col)
    got = spread(lse, "src", by_src)

    def body(*refs):
        second_rows(whole_s, whole_t, *refs)

    beta, mass = call(
        body, [(1, cols), (n_tgt, 8, rows // 8)], xt, slogw, tlogw, alpha, got, operands=by_row
    )
    got = spread(mass, "tgt", by_tgt)

    def body(*refs):
        second_cols(whole_t, *refs)

    alpha, sums = call(
        body, [(1, rows), col_row], xt, tlogw, alpha, beta, got, operands=by_col
    )
    got = spread(sums, "src", by_src)
    (means,) = call(share_means, [col_row], got)
    got = spread(means, "src", by_src)
    target_means, beta, sums = call(
        last_rows, [(features, cols), (1, cols), row_row], xt, alpha, beta, got, operands=by_row
    )
    got = spread(sums, "tgt", by_tgt)
    (means,) = call(share_means, [row_row], got)
    got = spread(means, "tgt", by_tgt)

    def body(*refs):
        finish_rows(whole_s, *refs)

    projected, ratio, pot_src, pulled, pot_tgt = call(
        body,
        [(features, rows), (1, rows), (1, rows), (features, cols), (1, cols)],
        xt,
        slogw,
        alpha,
        beta,
        target_means,
        got,
    )
    return (pot_src.reshape(rows), pot_tgt.reshape(cols), ratio.reshape(rows), projected, pulled)


def solution(mesh):
    in_specs = (P(None, "src"), P(None, "tgt"), P("src"), P("tgt"))
    out_specs = (P("src"), P("tgt"), P("src"), P(None, "src"), P(None, "tgt"))
    return jax.shard_map(
        per_device, mesh=mesh, in_specs=in_specs, out_specs=out_specs, check_vma=False
    )
```

```python
import math

import jax
import jax.numpy as jnp
from jax import lax
from jax.experimental import pallas as pl
from jax.experimental.pallas import tpu as pltpu
from jax.sharding import PartitionSpec as P

EPSILON = 0.1
LOG2E = math.log2(math.e)
KAPPA = LOG2E / EPSILON
LANES = 128
CHUNK = 256
LSE_CHUNK = 64
DEPTH = 64
HALF = 8
INNER = 8
FIRST = 5
STRIDE = 11
SAFE = 2.0**-80


def pieces(value):
    high = value.astype(jnp.bfloat16).astype(jnp.float32)
    rest = value - high
    mid = rest.astype(jnp.bfloat16).astype(jnp.float32)
    low = (rest - mid).astype(jnp.bfloat16).astype(jnp.float32)
    return high, mid, low


def tail_rows(count, dual, dual_first):
    row = lax.broadcasted_iota(jnp.int32, (16, count), 0)
    high, mid, low = pieces(dual)
    at = 0 if dual_first else 3
    ones_at = 3 - at
    out = jnp.where((row >= ones_at) & (row < ones_at + 3), 1.0, 0.0)
    out = jnp.where(row == at, high, out)
    out = jnp.where(row == at + 1, mid, out)
    return jnp.where(row == at + 2, low, out)


def fill_operands(a_points, a_dual, b_points, b_dual, a_ref, b_ref):
    features = a_points.shape[0]
    a = a_points.astype(jnp.float32)
    cross = 2.0 * KAPPA / features
    rows = jnp.concatenate([a, a, a, tail_rows(a.shape[1], a_dual, False)], axis=0)
    a_ref[...] = rows.T.astype(jnp.bfloat16)
    high, mid, low = pieces(b_points.astype(jnp.float32) * cross)
    b_ref[...] = jnp.concatenate(
        [high, mid, low, tail_rows(high.shape[1], b_dual, True)], axis=0
    ).astype(jnp.bfloat16)


def score_chunk(a_ref, b_ref, at, count):
    return jnp.dot(a_ref[at : at + count, :], b_ref[...], preferred_element_type=jnp.float32)


def pack(row):
    width = row.shape[1] // 8
    return jnp.concatenate([row[:, r * width : (r + 1) * width] for r in range(8)], axis=0)


def unpack(tile):
    return jnp.concatenate([tile[r : r + 1, :] for r in range(8)], axis=1)


def by_sublane(array):
    return array.reshape(array.shape[0] // 8, 8, array.shape[1])


def lse_columns(a_ref, b_ref, b_dual, out_ref):
    def store(lse):
        for d in range(out_ref.shape[0]):
            out_ref[d] = lse - pack(b_dual)

    total = pack(total_of(a_ref, b_ref))
    store(jnp.log(total) * LOG2E)

    @pl.when(jnp.min(total) < SAFE)
    def with_peaks():
        store(pack(lse_of(a_ref, b_ref)))


def lse_of(a_ref, b_ref):
    peak = None
    for at in range(0, a_ref.shape[0], LSE_CHUNK):
        scores = by_sublane(score_chunk(a_ref, b_ref, at, LSE_CHUNK))
        here = jnp.max(scores, axis=0)
        if peak is None:
            peak = here
            total = jnp.sum(jnp.exp2(scores - peak[None]), axis=0)
        else:
            risen = jnp.maximum(peak, here)
            total = total * jnp.exp2(peak - risen) + jnp.sum(
                jnp.exp2(scores - risen[None]), axis=0
            )
            peak = risen
    top = jnp.max(peak, axis=0, keepdims=True)
    total = jnp.sum(total * jnp.exp2(peak - top), axis=0, keepdims=True)
    return top + jnp.log(total) * LOG2E


def total_of(a_ref, b_ref):
    total = jnp.zeros((8, b_ref.shape[1]), jnp.float32)
    for at in range(0, a_ref.shape[0], CHUNK):
        total = total + jnp.sum(by_sublane(jnp.exp2(score_chunk(a_ref, b_ref, at, CHUNK))), axis=0)
    return jnp.sum(total, axis=0, keepdims=True)


def sum_columns(a_ref, b_ref, out_ref):
    total = pack(total_of(a_ref, b_ref))
    for d in range(out_ref.shape[0]):
        out_ref[d] = total


def weighted_columns(a_ref, b_ref, points_ref, out_ref, split):
    features = points_ref.shape[0]
    share = features // split
    cols = b_ref.shape[1]
    total = jnp.zeros((8, cols), jnp.float32)
    moved = jnp.zeros((features, cols), jnp.float32)
    for at in range(0, a_ref.shape[0], CHUNK):
        weight = jnp.exp2(score_chunk(a_ref, b_ref, at, CHUNK))
        total = total + jnp.sum(by_sublane(weight), axis=0)
        points = points_ref[:, at : at + CHUNK]
        rounded = weight.astype(jnp.bfloat16)
        moved = moved + jnp.dot(points, rounded, preferred_element_type=jnp.float32)
    total = jnp.sum(total, axis=0, keepdims=True)
    for q in range(cols // LANES):
        lanes = slice(q * LANES, (q + 1) * LANES)
        for h in range(split):
            d = q * split + h
            out_ref[d, :, 0:LANES] = total[:, lanes]
            for k in range(share):
                out_ref[d, :, (k + 1) * LANES : (k + 2) * LANES] = moved[
                    h * share + k : h * share + k + 1, lanes
                ]


def norm_of(points_ref):
    points = points_ref[...].astype(jnp.float32)
    return jnp.sum(points * points, axis=0, keepdims=True)


def joined_lse(got_ref):
    parts = [got_ref[d] for d in range(got_ref.shape[0])]
    top = parts[0]
    for part in parts[1:]:
        top = jnp.maximum(top, part)
    total = jnp.exp2(parts[0] - top)
    for part in parts[1:]:
        total = total + jnp.exp2(part - top)
    return top + jnp.log(total) * LOG2E


def joined_sum(got_ref):
    total = got_ref[0]
    for d in range(1, got_ref.shape[0]):
        total = total + got_ref[d]
    return total


def log2_weight(logw_ref, whole):
    return (logw_ref[...] - math.log(whole)) * LOG2E


def clouds(xt_ref):
    features = xt_ref.shape[0] // 2
    return xt_ref.at[:features], xt_ref.at[features:]


def norm_dual(points_ref):
    return norm_of(points_ref) * (-KAPPA / points_ref.shape[0])


def first_rows(xt_ref, out_ref, a_ref, b_ref):
    x_ref, t_ref = clouds(xt_ref)
    over = norm_dual(x_ref)
    fill_operands(t_ref[...], norm_dual(t_ref), x_ref[...], over, a_ref, b_ref)
    lse_columns(a_ref, b_ref, over, out_ref)


def first_cols(whole, xt_ref, logw_ref, got_ref, alpha_ref, out_ref, a_ref, b_ref):
    x_ref, t_ref = clouds(xt_ref)
    alpha = log2_weight(logw_ref, whole) - unpack(joined_lse(got_ref))
    alpha_ref[...] = alpha
    over = norm_dual(t_ref)
    fill_operands(x_ref[...], alpha, t_ref[...], over, a_ref, b_ref)
    lse_columns(a_ref, b_ref, over, out_ref)


def second_rows(
    whole_s, whole_t, xt_ref, slogw_ref, tlogw_ref, alpha_ref, got_ref, beta_ref, out_ref, a_ref, b_ref
):
    x_ref, t_ref = clouds(xt_ref)
    beta = log2_weight(tlogw_ref, whole_t) - unpack(joined_lse(got_ref))
    beta_ref[...] = beta
    over = alpha_ref[...] - log2_weight(slogw_ref, whole_s)
    fill_operands(t_ref[...], beta, x_ref[...], over, a_ref, b_ref)
    sum_columns(a_ref, b_ref, out_ref)


def second_cols(
    whole_t, xt_ref, tlogw_ref, alpha_ref, beta_ref, got_ref, alpha2_ref, out_ref, a_ref, b_ref
):
    x_ref, t_ref = clouds(xt_ref)
    alpha = alpha_ref[...] - unpack(jnp.log(joined_sum(got_ref)) * LOG2E)
    alpha2_ref[...] = alpha
    over = beta_ref[...] - log2_weight(tlogw_ref, whole_t)
    fill_operands(x_ref[...], alpha, t_ref[...], over, a_ref, b_ref)
    weighted_columns(a_ref, b_ref, x_ref, out_ref, x_ref.shape[0] // HALF)


def share_means(got_ref, out_ref):
    total = joined_sum(got_ref)
    mass = total[:, :LANES]
    for d in range(out_ref.shape[0]):
        out_ref[d, :, 0:LANES] = mass
    for at in range(LANES, total.shape[1], LANES):
        mean = total[:, at : at + LANES] / mass
        for d in range(out_ref.shape[0]):
            out_ref[d, :, at : at + LANES] = mean


def unpack_means(got_ref, means_ref, split):
    features = means_ref.shape[0]
    share = features // split
    masses = []
    for d in range(got_ref.shape[0]):
        q, h = divmod(d, split)
        if h == 0:
            masses.append(got_ref[d, :, 0:LANES])
        for k in range(share):
            means_ref[h * share + k : h * share + k + 1, q * LANES : (q + 1) * LANES] = got_ref[
                d, :, (k + 1) * LANES : (k + 2) * LANES
            ]
    return jnp.concatenate(masses, axis=1)


def last_rows(
    xt_ref, alpha_ref, beta_ref, got_ref, means_ref, beta2_ref, out_ref, a_ref, b_ref
):
    x_ref, t_ref = clouds(xt_ref)
    mass = unpack_means(got_ref, means_ref, x_ref.shape[0] // HALF)
    beta = beta_ref[...] - jnp.log(mass) * LOG2E
    beta2_ref[...] = beta
    fill_operands(t_ref[...], beta, x_ref[...], alpha_ref[...], a_ref, b_ref)
    weighted_columns(a_ref, b_ref, t_ref, out_ref, 1)


def finish_rows(
    whole,
    xt_ref,
    logw_ref,
    alpha_ref,
    beta_ref,
    means_ref,
    got_ref,
    projected_ref,
    ratio_ref,
    pot_src_ref,
    pulled_ref,
    pot_tgt_ref,
):
    x_ref, t_ref = clouds(xt_ref)
    pulled_ref[...] = means_ref[...]
    pot_tgt_ref[...] = beta_ref[...] * (1.0 / KAPPA) + norm_of(t_ref) * (1.0 / t_ref.shape[0])
    mass = unpack_means(got_ref, projected_ref, 1)
    ratio_ref[...] = mass * jnp.exp(math.log(whole) - logw_ref[...]) - 1.0
    pot_src_ref[...] = alpha_ref[...] * (1.0 / KAPPA) + norm_of(x_ref) * (1.0 / x_ref.shape[0])


def call(body, outs, *args, operands=None):
    scratch = []
    if operands is not None:
        scratch = [
            pltpu.VMEM((operands[0], DEPTH), jnp.bfloat16),
            pltpu.VMEM((DEPTH, operands[1]), jnp.bfloat16),
        ]
    return pl.pallas_call(
        body,
        out_shape=[jax.ShapeDtypeStruct(shape, jnp.float32) for shape in outs],
        scratch_shapes=scratch,
        compiler_params=pltpu.CompilerParams(vmem_limit_bytes=48 * 1024 * 1024),
    )(*args)


def spread(parts, axis, order):
    return lax.all_to_all(parts, axis, 0, 0, axis_index_groups=[order], tiled=True)


def per_device(x, t, source_logw, target_logw):
    features, rows = x.shape
    cols = t.shape[1]
    n_src, n_tgt = lax.axis_size("src"), lax.axis_size("tgt")
    whole_s, whole_t = rows * n_src, cols * n_tgt
    slogw = source_logw.reshape(1, rows)
    tlogw = target_logw.reshape(1, cols)
    split = features // HALF
    xt = jnp.concatenate([x, t], axis=0)
    outer = n_src // INNER
    by_src = [(r + outer // 2) % outer * INNER + (r // outer + FIRST) % INNER for r in range(n_src)]
    by_tgt = [(STRIDE * r + n_tgt // 2) % n_tgt for r in range(n_tgt)]
    assert rows == cols and n_src * LANES == cols * split and n_tgt * LANES == rows
    col_row = (n_src, 1, (HALF + 1) * LANES)
    row_row = (n_tgt, 1, (features + 1) * LANES)
    by_row, by_col = (cols, rows), (rows, cols)

    (lse,) = call(first_rows, [(n_tgt, 8, rows // 8)], xt, operands=by_row)
    got = spread(lse, "tgt", by_tgt)

    def body(*refs):
        first_cols(whole_s, *refs)

    alpha, lse = call(body, [(1, rows), (n_src, 8, cols // 8)], xt, slogw, got, operands=by_col)
    got = spread(lse, "src", by_src)

    def body(*refs):
        second_rows(whole_s, whole_t, *refs)

    beta, mass = call(
        body, [(1, cols), (n_tgt, 8, rows // 8)], xt, slogw, tlogw, alpha, got, operands=by_row
    )
    got = spread(mass, "tgt", by_tgt)

    def body(*refs):
        second_cols(whole_t, *refs)

    alpha, sums = call(
        body, [(1, rows), col_row], xt, tlogw, alpha, beta, got, operands=by_col
    )
    got = spread(sums, "src", by_src)
    (means,) = call(share_means, [col_row], got)
    got = spread(means, "src", by_src)
    target_means, beta, sums = call(
        last_rows, [(features, cols), (1, cols), row_row], xt, alpha, beta, got, operands=by_row
    )
    got = spread(sums, "tgt", by_tgt)
    (means,) = call(share_means, [row_row], got)
    got = spread(means, "tgt", by_tgt)

    def body(*refs):
        finish_rows(whole_s, *refs)

    projected, ratio, pot_src, pulled, pot_tgt = call(
        body,
        [(features, rows), (1, rows), (1, rows), (features, cols), (1, cols)],
        xt,
        slogw,
        alpha,
        beta,
        target_means,
        got,
    )
    return (pot_src.reshape(rows), pot_tgt.reshape(cols), ratio.reshape(rows), projected, pulled)


def solution(mesh):
    in_specs = (P(None, "src"), P(None, "tgt"), P("src"), P("tgt"))
    out_specs = (P("src"), P("tgt"), P("src"), P(None, "src"), P(None, "tgt"))
    return jax.shard_map(
        per_device, mesh=mesh, in_specs=in_specs, out_specs=out_specs, check_vma=False
    )
```
